32 devices in a mesh: groups: 2 (over y), sector: 4 (over z), contr: 2 (over x), mpo: 2 (over core).
Axes of the slice: x: 2, y: 2, z: 4, core: 2. Of those that a mesh axis runs over, the one named last changes fastest.
Arguments:
- psi: bfloat16 [8, 4, 256, 256], P(('groups', 'sector'), None, 'contr'), parts along dimension 0, may hold values from -6 to 6
- sector_size: int32 [8, 4], P(('groups', 'sector')), parts along dimension 0, may hold values from 64 to 256, as said below
- left_env: bfloat16 [26, 8, 4, 256, 256], P('mpo', ('groups', 'sector'), None, 'contr'), parts along dimension 1
- right_env: bfloat16 [26, 8, 4, 256, 256], P('mpo', ('groups', 'sector'), None, None, 'contr'), parts along dimension 1
- term_shift: int32 [52], P(('groups', 'mpo')), parts along dimension 0, may hold values from 0 to 4
Outputs:
- first_image: bfloat16 [8, 4, 256, 256], P(('groups', 'sector'), None, 'contr'), parts along dimension 0
- second_image: bfloat16 [8, 4, 256, 256], P(('groups', 'sector'), None, 'contr'), parts along dimension 0
- ritz_value: float32 [2], P('groups'), parts along dimension 0
The draws below stay inside these ranges and needn't reach their ends.
There are 2 independent parts, one for each index of `groups`. The reference program is written for one: setup_inputs(seed, part) draws one part's arguments, and reference() takes and returns one part's arrays. A program takes and returns all parts, laid end to end along the dimension named above; each array names one. Nothing has to cross between parts.
Inputs may be any that keep to these rules, and one draw needn't show every extreme that they name: `sector_size`: some sector has live size 256 and some has 64.
All inputs are finite; a program needn't handle non-finite values.
Results may differ from the reference program's by a relative error of at most 0.0024.
The reference program's roundings to bfloat16 on the way count: a program that leaves them out, or rounds other values in their place, can miss the bound.
Values may be sent and summed in bfloat16 or wider, within the bound.
No kernel may reach another device: no remote copies, remote signals or barrier semaphores. Data moves between devices by JAX's collectives and lax.ppermute only.
A program may use at most 64 MiB of HBM per device.

```python
import jax
import jax.numpy as jnp
from jax import lax

SB = 256
NW = 26
QD = 4
NU = 4


def identity_part():
    rows = jnp.arange(SB, dtype=jnp.int32)
    return (rows[:, None] == rows[None, :]).astype(jnp.float32)


def draw_term_shift(key, part):
    key = jax.random.fold_in(key, 11)
    return (jax.random.permutation(key, NW) % 5).astype(jnp.int32)


def draw_sector_size(key, part):
    key = jax.random.fold_in(key, 12)
    first_key, second_key, third_key = jax.random.split(key, 3)
    total = NU * QD
    sizes = jax.random.randint(first_key, (total,), SB // 4, SB + 1)
    top_slot = jax.random.randint(second_key, (), 0, total)
    low_slot = (top_slot + 1 + jax.random.randint(third_key, (), 0, total - 1)) % total
    slots = jnp.arange(total, dtype=jnp.int32)
    sizes = jnp.where(slots == top_slot, SB, sizes)
    sizes = jnp.where(slots == low_slot, SB // 4, sizes)
    return sizes.reshape(NU, QD).astype(jnp.int32)


def draw_left_env(key, part):
    key = jax.random.fold_in(key, 13)
    noise_key = jax.random.fold_in(key, 0)
    shape = (NW, NU, QD, SB, SB)
    noise = jax.random.normal(noise_key, shape, jnp.float32)
    return (identity_part() + noise / jnp.sqrt(float(SB))).astype(jnp.bfloat16)


def draw_right_env(key, part):
    key = jax.random.fold_in(key, 14)
    noise_key = jax.random.fold_in(key, 0)
    shape = (NW, NU, QD, SB, SB)
    noise = jax.random.normal(noise_key, shape, jnp.float32)
    return ((identity_part() + noise / jnp.sqrt(float(SB))) / jnp.sqrt(float(NW))).astype(jnp.bfloat16)


def steps_of(key, dims, shards, smallest, top_value):
    def one(axis_at, shards_of):
        heights = jax.random.uniform(jax.random.fold_in(jax.random.fold_in(key, 6), axis_at), (shards_of,), jnp.float32, smallest / len(shards), top_value / len(shards))
        return jnp.repeat(jnp.exp(heights), dims[axis_at] // shards_of).reshape((-1,) + (1,) * (len(dims) - axis_at - 1))

    loudness = one(*shards[0])
    for cut in shards[1:]:
        loudness = loudness * one(*cut)
    return loudness


def centred(stream_key, extent, scale, limit, pieces=(), kind=jnp.bfloat16):
    factor_of = steps_of(stream_key, extent, pieces, -0.22, 0.18) if pieces else 1.0
    result = jax.random.normal(stream_key, extent, jnp.float32) * scale * factor_of
    return jnp.minimum(jnp.maximum(result, -limit), limit).astype(kind)


def setup_inputs(seed: int = 0, part: int = 0) -> dict:
    arg_keys = jax.random.split(jax.random.key(seed), 6)
    part_splits = jax.random.split(jax.random.fold_in(arg_keys[5], part), 6)
    psi = centred(part_splits[0], (NU, QD, SB, SB), 1.0, 6.0, ((0, 4), (2, 2)))
    sector_size = draw_sector_size(jax.random.fold_in(jax.random.fold_in(arg_keys[5], part), 71), part)
    left_env = draw_left_env(jax.random.fold_in(jax.random.fold_in(arg_keys[5], part), 71), part)
    right_env = draw_right_env(jax.random.fold_in(jax.random.fold_in(arg_keys[5], part), 71), part)
    term_shift = draw_term_shift(jax.random.fold_in(jax.random.fold_in(arg_keys[5], part), 71), part)
    return {"psi": psi, "sector_size": sector_size, "left_env": left_env, "right_env": right_env, "term_shift": term_shift}


def live_mask(sector_size):
    index = jnp.arange(SB, dtype=jnp.int32)
    sizes = sector_size[:, :, None, None]
    inside = (index[None, None, :, None] < sizes) & (index[None, None, None, :] < sizes)
    return inside.astype(jnp.float32)

def shifted_sources(field):
    count_u = field.shape[0]
    count_v = field.shape[1]
    padded = jnp.pad(field, ((1, 1), (1, 1), (0, 0), (0, 0)))
    return jnp.stack([field, padded[0:count_u, 1:count_v + 1], padded[2:count_u + 2, 1:count_v + 1], padded[1:count_u + 1, 0:count_v], padded[1:count_u + 1, 2:count_v + 2]])

def apply_h(field, left_env, right_env, term_shift, mask):
    stacked = shifted_sources(field)

    def one_sector(index_u):
        sources = stacked[term_shift, index_u].astype(jnp.float32)
        blocks = left_env[:, index_u].astype(jnp.float32)
        inner = jnp.einsum('wvrl,wvml->wvrm', sources, blocks).astype(jnp.bfloat16)
        return jnp.einsum('wvpr,wvrm->vpm', right_env[:, index_u].astype(jnp.float32), inner.astype(jnp.float32))
    return lax.map(one_sector, jnp.arange(field.shape[0], dtype=jnp.int32)) * mask

def reference(psi, sector_size, left_env, right_env, term_shift):
    mask = live_mask(sector_size)
    first = psi * mask.astype(jnp.bfloat16)
    image_one = apply_h(first, left_env, right_env, term_shift, mask)
    trial = first.astype(jnp.float32)
    product = jnp.sum(trial * image_one)
    squares = jnp.sum(trial * trial)
    ritz_value = product / (squares + 1e-06)
    resid = image_one - ritz_value * trial
    factor = lax.rsqrt(jnp.mean(resid * resid) + 1e-06)
    second = (resid * factor).astype(jnp.bfloat16)
    image_two = apply_h(second, left_env, right_env, term_shift, mask)
    return (image_one.astype(jnp.bfloat16), image_two.astype(jnp.bfloat16), jnp.reshape(ritz_value, (1,)))
```

```python
import functools

import jax
import jax.numpy as jnp
from jax import lax
from jax.experimental import pallas as pl
from jax.experimental.pallas import tpu as pltpu
from jax.sharding import PartitionSpec as P

CHUNKS = (4, 4, 3, 2)
EPS = 1e-06


def padded(cells, sides, width):
    for axis, dim in sides:
        count = lax.axis_size(axis)
        ends = count - 1
        head = lax.slice_in_dim(cells, 0, width, axis=dim)
        tail = lax.slice_in_dim(cells, cells.shape[dim] - width, cells.shape[dim], axis=dim)
        cells = jnp.concatenate(
            [
                lax.ppermute(tail, axis, [(i, (i + 1) % count) for i in range(ends)]),
                cells,
                lax.ppermute(head, axis, [((i + 1) % count, i) for i in range(ends)]),
            ],
            axis=dim,
        )
    return cells


def on_device_gather(psi, sector_size, left_env, right_env, term_shift):
    slots = psi.shape[1]
    rows_here = psi.shape[2]
    width = psi.shape[3]
    row_ids = lax.axis_index("contr") * rows_here + lax.iota(jnp.int32, rows_here)
    col_ids = lax.iota(jnp.int32, width)
    live = sector_size[0][:, None, None]
    mask = ((row_ids[None, :, None] < live) & (col_ids[None, None, :] < live)).astype(jnp.float32)[
        None
    ]

    def apply_h(field):
        extended = padded(field, (("sector", 0),), 1)
        own = field[0]
        blank = jnp.zeros_like(own[:1])
        stacked = jnp.stack(
            [
                own,
                extended[0],
                extended[2],
                jnp.concatenate([blank, own[:-1]], 0),
                jnp.concatenate([own[1:], blank], 0),
            ]
        )
        sources = stacked[term_shift]
        inner = jnp.einsum(
            "wvrl,wvml->wvrm",
            sources,
            lax.all_gather(left_env, "contr", axis=3, tiled=True)[:, 0],
            preferred_element_type=jnp.float32,
        ).astype(jnp.bfloat16)
        partial_sum = jnp.einsum(
            "wvpr,wvrm->vpm", right_env[:, 0], inner, preferred_element_type=jnp.float32
        )
        summed = lax.psum_scatter(partial_sum, "contr", scatter_dimension=1, tiled=True)
        summed = lax.psum(summed, "mpo")
        return summed[None] * mask

    first = psi * mask.astype(jnp.bfloat16)
    image_one = apply_h(first)
    trial = first.astype(jnp.float32)
    entries = float(lax.axis_size("sector") * slots * width * width)
    product, squares = lax.psum(
        (jnp.sum(trial * image_one), jnp.sum(trial * trial)), ("sector", "contr")
    )
    ritz_value = product / (squares + EPS)
    resid = image_one - ritz_value * trial
    total_sq = lax.psum(jnp.sum(resid * resid), ("sector", "contr"))
    factor = lax.rsqrt(total_sq / entries + EPS)
    second = (resid * factor).astype(jnp.bfloat16)
    image_two = apply_h(second)
    return (
        image_one.astype(jnp.bfloat16),
        image_two.astype(jnp.bfloat16),
        jnp.reshape(ritz_value, (1,)),
    )


def live_block(shape, live):
    rows = lax.broadcasted_iota(jnp.int32, shape, 0)
    cols = lax.broadcasted_iota(jnp.int32, shape, 1)
    return (rows < live) & (cols < live)


def term(source, left, right):
    inner = lax.dot_general(
        source, left, (((1,), (1,)), ((), ())), preferred_element_type=jnp.float32
    ).astype(jnp.bfloat16)
    return jnp.dot(right, inner, preferred_element_type=jnp.float32)


def first_kernel(start, stop, last, info, *refs):
    (l_own, r_own, l_core, r_core, l_side, r_side, l_diag, r_diag, source) = refs[:9]
    refs = refs[9:]
    if start:
        before, refs = refs[0], refs[3:]
    left, right, total = refs[:3]
    step = pl.program_id(0)
    half = l_side.shape[1]
    mine = pl.multiple_of(info[0] * half, half)
    theirs = pl.multiple_of((1 - info[0]) * half, half)

    @pl.when(step == 0)
    def _():
        total[...] = before[...] if start else jnp.zeros_like(total)

    halves = (
        (l_own[0, 0, 0], r_own[0, 0, 0], l_side[0], r_side[0]),
        (l_core[0], r_core[0], l_diag[0], r_diag[0]),
    )
    terms = pl.num_programs(0)
    sums = None
    for core, (left_a, right_a, left_b, right_b) in enumerate(halves):
        left[0, core, pl.ds(mine, half), :] = left_a
        left[0, core, pl.ds(theirs, half), :] = left_b
        right[0, core, :, pl.ds(mine, half)] = right_a
        right[0, core, :, pl.ds(theirs, half)] = right_b
        shift = info[3 + core * info[2] + start + step]
        part = term(source[shift], left[0, core], right[0, core])
        sums = part if sums is None else sums + part
    total[...] += sums
    if last:
        image, stats = refs[3:5]

        @pl.when(step == terms - 1)
        def _():
            field = source[0].astype(jnp.float32)
            block = jnp.where(live_block(field.shape, info[1]), total[...], 0.0)
            image[...] = block.astype(image.dtype)
            total[...] = block
            product = jnp.sum(field * block, keepdims=True)
            squares = jnp.sum(field * field, keepdims=True)
            quotient = product / (squares + EPS)
            resid = block - quotient * field
            rest = jnp.sum(resid * resid, keepdims=True)
            lanes = stats.shape[1]
            for row, value in enumerate((product, squares, rest, quotient)):
                stats[row : row + 1, :] = jnp.broadcast_to(value, (1, lanes))


def second_kernel(entries, info, left, right, blocks, source, stats, image, ritz, second, total):
    step = pl.program_id(0)

    @pl.when(step == 0)
    def _():
        count, slots = stats.shape[:2]
        tiles = []
        for u in range(count):
            shift = lax.rem(info[0] - u + count, count)
            for v in range(slots):
                tiles.append(stats[shift, info[1] ^ v])
        product = sum(t[0:1] for t in tiles)
        squares = sum(t[1:2] for t in tiles)
        quotient = product / (squares + EPS)
        rest = jnp.zeros_like(quotient)
        for t in tiles:
            off = t[3:4] - quotient
            cross = t[0:1] - t[3:4] * t[1:2]
            rest += t[2:3] + 2.0 * off * cross + off * off * t[1:2]
        factor = lax.rsqrt(rest / entries + EPS)
        ritz[...] = jnp.broadcast_to(quotient, ritz.shape)
        for place, block in enumerate(blocks):
            resid = block[...] - quotient[:, :1] * source[place].astype(jnp.float32)
            second[place] = (resid * factor[:, :1]).astype(jnp.bfloat16)
        total[...] = jnp.zeros_like(total)

    cores = left.shape[1]
    sums = None
    for core in range(cores):
        shift = info[3 + core * pl.num_programs(0) + step]
        part = term(second[shift], left[0, core], right[0, core])
        sums = part if sums is None else sums + part
    total[...] += sums

    @pl.when(step == pl.num_programs(0) - 1)
    def _():
        live = live_block(total.shape, info[2])
        image[...] = jnp.where(live, total[...], 0.0).astype(image.dtype)


def on_device(psi, sector_size, left_env, right_env, term_shift):
    terms, _, slots, half, width = left_env.shape
    cell = ("contr", "mpo")
    across, core = lax.axis_index("contr"), lax.axis_index("mpo")
    me = across * 2 + core
    sector = lax.axis_index("sector")
    sectors = lax.axis_size("sector")

    def swap(array, flip):
        return lax.ppermute(array, cell, [(i, i ^ flip) for i in range(slots)])

    def pick(array, flip, start, stop):
        part = lax.slice_in_dim(array, start, stop, axis=0)[:, 0]
        return lax.dynamic_index_in_dim(part, me ^ flip, 1, keepdims=False)

    psi_theirs = swap(lax.dynamic_slice_in_dim(psi[0], 1 - across, 3, axis=0), 2)
    psi_mine = lax.dynamic_slice_in_dim(psi[0], across, 3, axis=0)
    shift_core = swap(term_shift, 1)
    chunks = []
    start = 0
    for size in CHUNKS:
        stop = start + size
        chunks.append(
            (start, stop)
            + tuple(
                swap(pick(env, flip, start, stop), flip)
                for flip in (2, 3)
                for env in (left_env, right_env)
            )
        )
        start = stop
    left_core = swap(pick(left_env, 1, 0, terms), 1)
    right_core = swap(pick(right_env, 1, 0, terms), 1)

    whole = jnp.where(
        across == 0,
        jnp.concatenate([psi_mine, psi_theirs], axis=1),
        jnp.concatenate([psi_theirs, psi_mine], axis=1),
    )
    sizes = lax.dynamic_slice_in_dim(sector_size[0], across, 3, axis=0)[:, None, None]
    ids = lax.iota(jnp.int32, width)
    live = (ids[None, :, None] < sizes) & (ids[None, None, :] < sizes)
    whole = jnp.where(live, whole, jnp.zeros_like(whole))
    blank = jnp.zeros_like(whole[:1])
    framed = jnp.concatenate([blank, whole, blank], axis=0)
    own = lax.dynamic_index_in_dim(whole, me - across, 0, keepdims=False)
    up = [(i, i + 1) for i in range(sectors - 1)]
    down = [(i + 1, i) for i in range(sectors - 1)]
    source = jnp.stack(
        [
            own,
            lax.ppermute(own, "sector", up),
            lax.ppermute(own, "sector", down),
            lax.dynamic_index_in_dim(framed, me - across, 0, keepdims=False),
            lax.dynamic_index_in_dim(framed, me - across + 2, 0, keepdims=False),
        ]
    )
    size_here = lax.dynamic_index_in_dim(sector_size[0], me, 0, keepdims=False)
    shifts = jnp.concatenate([term_shift, shift_core])
    info = jnp.concatenate(
        [jnp.stack([across, size_here, jnp.int32(terms), me]).astype(jnp.int32)[:3], shifts, me[None]]
    )
    spot = info.shape[0] - 1

    kept = None
    both = jax.ShapeDtypeStruct((terms, 2, width, width), jnp.bfloat16)
    plain = jax.ShapeDtypeStruct((width, width), jnp.float32)
    flat = pl.BlockSpec((width, width), lambda i, s: (0, 0))
    for start, stop, l_side, r_side, l_diag, r_diag in chunks:
        last = stop == terms
        pair = pl.BlockSpec((1, 2, width, width), lambda i, s, at=start: (at + i, 0, 0, 0))
        l_row = lambda at: pl.BlockSpec((1, half, width), lambda i, s, at=at: (at + i, 0, 0))
        r_row = lambda at: pl.BlockSpec((1, width, half), lambda i, s, at=at: (at + i, 0, 0))
        in_specs = [
            pl.BlockSpec((1, 1, 1, half, width), lambda i, s, at=start: (at + i, 0, s[spot], 0, 0)),
            pl.BlockSpec((1, 1, 1, width, half), lambda i, s, at=start: (at + i, 0, s[spot], 0, 0)),
            l_row(start),
            r_row(start),
            l_row(0),
            r_row(0),
            l_row(0),
            r_row(0),
            pl.BlockSpec((5, width, width), lambda i, s: (0, 0, 0)),
        ]
        operands = [left_env, right_env, left_core, right_core, l_side, r_side, l_diag, r_diag, source]
        aliases = {}
        if start:
            in_specs += [flat, pl.BlockSpec(memory_space=pl.ANY), pl.BlockSpec(memory_space=pl.ANY)]
            operands += [kept[2], kept[0], kept[1]]
            aliases = {11: 0, 12: 1}
        out_shape = [both, both, plain]
        out_specs = [pair, pair, flat]
        if last:
            out_shape += [
                jax.ShapeDtypeStruct((width, width), jnp.bfloat16),
                jax.ShapeDtypeStruct((8, 128), jnp.float32),
            ]
            out_specs += [flat, pl.BlockSpec((8, 128), lambda i, s: (0, 0))]
        flops = 8 * (stop - start) * width**3
        kept = pl.pallas_call(
            functools.partial(first_kernel, start, stop, last),
            grid_spec=pltpu.PrefetchScalarGridSpec(
                num_scalar_prefetch=1,
                grid=(stop - start,),
                in_specs=in_specs,
                out_specs=out_specs,
            ),
            out_shape=out_shape,
            input_output_aliases=aliases,
            compiler_params=pltpu.CompilerParams(vmem_limit_bytes=32 * 2**20),
            cost_estimate=pl.CostEstimate(
                flops=flops, bytes_accessed=(stop - start) * 2**20, transcendentals=0
            ),
            name=f"first_terms_{start}",
        )(info, *operands)
    left_all, right_all, image_one, first_here, stats = kept

    slot_up = [(i, i + 1) for i in range(slots - 1)]
    slot_down = [(i + 1, i) for i in range(slots - 1)]
    blocks = [
        image_one,
        lax.ppermute(image_one, "sector", up),
        lax.ppermute(image_one, "sector", down),
        lax.ppermute(image_one, cell, slot_up),
        lax.ppermute(image_one, cell, slot_down),
    ]
    stats = jnp.stack([stats, swap(stats, 1), swap(stats, 2), swap(stats, 3)])
    stats = jnp.stack(
        [stats]
        + [
            lax.ppermute(stats, "sector", [(i, (i + d) % sectors) for i in range(sectors)])
            for d in range(1, sectors)
        ]
    )

    info_two = jnp.concatenate(
        [jnp.stack([sector, me, size_here]).astype(jnp.int32), shifts]
    )
    pair = pl.BlockSpec((1, 2, width, width), lambda i, s: (i, 0, 0, 0))
    entries = float(sectors * slots * width * width)
    second_here, ritz = pl.pallas_call(
        lambda info, left, right, b0, b1, b2, b3, b4, *refs: second_kernel(
            entries, info, left, right, (b0, b1, b2, b3, b4), *refs
        ),
        grid_spec=pltpu.PrefetchScalarGridSpec(
            num_scalar_prefetch=1,
            grid=(terms,),
            in_specs=[pair, pair]
            + [flat] * 5
            + [
                pl.BlockSpec((5, width, width), lambda i, s: (0, 0, 0)),
                pl.BlockSpec(stats.shape, lambda i, s: (0, 0, 0, 0)),
            ],
            out_specs=[flat, pl.BlockSpec((8, 128), lambda i, s: (0, 0))],
            scratch_shapes=[
                pltpu.VMEM((5, width, width), jnp.bfloat16),
                pltpu.VMEM((width, width), jnp.float32),
            ],
        ),
        out_shape=[
            jax.ShapeDtypeStruct((width, width), jnp.bfloat16),
            jax.ShapeDtypeStruct((8, 128), jnp.float32),
        ],
        compiler_params=pltpu.CompilerParams(vmem_limit_bytes=32 * 2**20),
        cost_estimate=pl.CostEstimate(
            flops=8 * terms * width**3, bytes_accessed=terms * 2**19, transcendentals=0
        ),
        name="second_terms",
    )(info_two, left_all, right_all, *blocks, source, stats)

    def spread(block):
        halves = block.reshape(2, half, width)
        mine = lax.dynamic_index_in_dim(halves, across, 0, keepdims=False)
        theirs = lax.dynamic_index_in_dim(halves, 1 - across, 0, keepdims=False)
        got = jnp.stack([mine, swap(mine, 1), swap(theirs, 2), swap(theirs, 3)])
        return got[me ^ lax.iota(jnp.int32, slots)][None]

    return spread(first_here), spread(second_here), ritz[0, :1]


def solution(mesh):
    fits = mesh.shape["contr"] == 2 and mesh.shape["mpo"] == 2

    def body(psi, sector_size, left_env, right_env, term_shift):
        run = on_device if fits and psi.shape[1] == 4 else on_device_gather
        return run(psi, sector_size, left_env, right_env, term_shift)

    return jax.shard_map(
        body,
        mesh=mesh,
        in_specs=(
            P(("groups", "sector"), None, "contr", None),
            P(("groups", "sector"), None),
            P("mpo", ("groups", "sector"), None, "contr", None),
            P("mpo", ("groups", "sector"), None, None, "contr"),
            P(("groups", "mpo")),
        ),
        out_specs=(
            P(("groups", "sector"), None, "contr", None),
            P(("groups", "sector"), None, "contr", None),
            P("groups"),
        ),
        check_vma=False,
    )
```

```python
import functools

import jax
import jax.numpy as jnp
from jax import lax
from jax.experimental import pallas as pl
from jax.experimental.pallas import tpu as pltpu
from jax.sharding import PartitionSpec as P

CUTS = (0, 4, 8, 11, 13)
EPS = 1e-06


def padded(cells, sides, width):
    for axis, dim in sides:
        count = lax.axis_size(axis)
        ends = count - 1
        head = lax.slice_in_dim(cells, 0, width, axis=dim)
        tail = lax.slice_in_dim(cells, cells.shape[dim] - width, cells.shape[dim], axis=dim)
        cells = jnp.concatenate(
            [
                lax.ppermute(tail, axis, [(i, (i + 1) % count) for i in range(ends)]),
                cells,
                lax.ppermute(head, axis, [((i + 1) % count, i) for i in range(ends)]),
            ],
            axis=dim,
        )
    return cells


def on_device_gather(psi, sector_size, left_env, right_env, term_shift):
    slots = psi.shape[1]
    rows_here = psi.shape[2]
    width = psi.shape[3]
    row_ids = lax.axis_index("contr") * rows_here + lax.iota(jnp.int32, rows_here)
    col_ids = lax.iota(jnp.int32, width)
    live = sector_size[0][:, None, None]
    mask = ((row_ids[None, :, None] < live) & (col_ids[None, None, :] < live)).astype(jnp.float32)[
        None
    ]

    def apply_h(field):
        extended = padded(field, (("sector", 0),), 1)
        own = field[0]
        blank = jnp.zeros_like(own[:1])
        stacked = jnp.stack(
            [
                own,
                extended[0],
                extended[2],
                jnp.concatenate([blank, own[:-1]], 0),
                jnp.concatenate([own[1:], blank], 0),
            ]
        )
        sources = stacked[term_shift]
        inner = jnp.einsum(
            "wvrl,wvml->wvrm",
            sources,
            lax.all_gather(left_env, "contr", axis=3, tiled=True)[:, 0],
            preferred_element_type=jnp.float32,
        ).astype(jnp.bfloat16)
        partial_sum = jnp.einsum(
            "wvpr,wvrm->vpm", right_env[:, 0], inner, preferred_element_type=jnp.float32
        )
        summed = lax.psum_scatter(partial_sum, "contr", scatter_dimension=1, tiled=True)
        summed = lax.psum(summed, "mpo")
        return summed[None] * mask

    first = psi * mask.astype(jnp.bfloat16)
    image_one = apply_h(first)
    trial = first.astype(jnp.float32)
    entries = float(lax.axis_size("sector") * slots * width * width)
    product, squares = lax.psum(
        (jnp.sum(trial * image_one), jnp.sum(trial * trial)), ("sector", "contr")
    )
    ritz_value = product / (squares + EPS)
    resid = image_one - ritz_value * trial
    total_sq = lax.psum(jnp.sum(resid * resid), ("sector", "contr"))
    factor = lax.rsqrt(total_sq / entries + EPS)
    second = (resid * factor).astype(jnp.bfloat16)
    image_two = apply_h(second)
    return (
        image_one.astype(jnp.bfloat16),
        image_two.astype(jnp.bfloat16),
        jnp.reshape(ritz_value, (1,)),
    )


def live_block(shape, start, live):
    rows = (lax.broadcasted_iota(jnp.int32, shape, 0) + start) % shape[0]
    cols = lax.broadcasted_iota(jnp.int32, shape, 1)
    return (rows < live) & (cols < live)


def fetch(pairs, sems):
    copies = [pltpu.make_async_copy(x, y, sems.at[n]) for n, (x, y) in enumerate(pairs)]
    for copy in copies:
        copy.start()
    done = [0]

    def until(count):
        for copy in copies[done[0] : count]:
            copy.wait()
        done[0] = max(done[0], count)

    return until


def pack_kernel(parts, info, left_env, right_env, *refs):
    count = len(parts)
    refs = refs[-2 * count - 2 :]
    outs, bufs, (ins_sem, outs_sem) = refs[:count], refs[count : 2 * count], refs[-2:]
    half = right_env.shape[-1]
    width = right_env.shape[-2]
    copies = []
    for (start, stop, flip), buf in zip(parts, bufs):
        slot = info[2] ^ flip
        span = pl.ds(start, stop - start)
        pieces = [(right_env.at[span, 0, slot], buf.at[:, pl.ds(0, width)])]
        for lane in range(width // half):
            pieces.append(
                (
                    left_env.at[span, 0, slot, :, pl.ds(lane * half, half)],
                    buf.at[:, pl.ds(width + lane * half, half)],
                )
            )
        copies.append(pieces)
    flat = [pair for pieces in copies for pair in pieces]
    until = fetch(flat, ins_sem)
    sends = [pltpu.make_async_copy(b, o, outs_sem.at[n]) for n, (b, o) in enumerate(zip(bufs, outs))]
    each = len(copies[0])
    for n, send in enumerate(sends):
        until(each * (n + 1))
        send.start()
    for send in sends:
        send.wait()


def pack(parts, info, left_env, right_env, after=()):
    width, half = right_env.shape[-2:]
    shapes = [(stop - start, 2 * width, half) for start, stop, _ in parts]
    out_shape = [jax.ShapeDtypeStruct(shape, jnp.bfloat16) for shape in shapes]
    size = sum(shape[0] for shape in shapes) * width * half * 8
    return pl.pallas_call(
        functools.partial(pack_kernel, parts),
        in_specs=[pl.BlockSpec(memory_space=pltpu.SMEM)]
        + [pl.BlockSpec(memory_space=pl.ANY)] * (2 + len(after)),
        out_specs=[pl.BlockSpec(memory_space=pl.ANY)] * len(parts),
        out_shape=out_shape,
        scratch_shapes=[pltpu.VMEM(shape, jnp.bfloat16) for shape in shapes]
        + [
            pltpu.SemaphoreType.DMA((len(parts) * (1 + width // half),)),
            pltpu.SemaphoreType.DMA((len(parts),)),
        ],
        compiler_params=pltpu.CompilerParams(vmem_limit_bytes=63 * 2**20),
        cost_estimate=pl.CostEstimate(flops=0, bytes_accessed=size, transcendentals=0),
        name=f"pack_{parts[0][0]}_{len(parts)}",
    )(info, left_env, right_env, *after)


def inner_block(source, near, far):
    half = near.shape[1]
    left = [
        jnp.concatenate([m[2 * half + k * half : 3 * half + k * half] for k in range(2)], axis=1)
        for m in (near, far)
    ]
    return lax.dot_general(
        source,
        jnp.concatenate(left, axis=0),
        (((1,), (1,)), ((), ())),
        preferred_element_type=jnp.float32,
    ).astype(jnp.bfloat16)


def add_terms(items, source, kept, group):
    width = source.shape[-1]
    half = width // 2
    total = None
    groups = [items[at : at + group] for at in range(0, len(items), group)]

    def inners(index):
        for k, (shift, near, far, i, j) in enumerate(groups[index]):
            kept[index % 2, k * width : (k + 1) * width, :] = inner_block(
                source[shift], near[i], far[j]
            )

    inners(0)
    for index, batch in enumerate(groups):
        if index + 1 < len(groups):
            inners(index + 1)
        right = jnp.concatenate(
            [m[n, :width] for _, near, far, i, j in batch for m, n in ((near, i), (far, j))], axis=1
        )
        part = jnp.dot(
            right,
            kept[index % 2, : len(batch) * width, :],
            preferred_element_type=jnp.float32,
        )
        total = part if total is None else total + part
    return total


def own_first(block, across):
    half = block.shape[0] // 2
    turned = jnp.concatenate([block[half:], block[:half]], axis=0)
    turned = jnp.concatenate([turned[:, half:], turned[:, :half]], axis=1)
    return jnp.where(across == 0, block, turned)


def first_kernel(start, stop, last, info, *refs):
    count = 6 if start else 5
    here, refs = refs[:count], refs[count:]
    outs, (sems, kept, *bufs) = refs[: 4 if last else 1], refs[4 if last else 1 :]
    own, core, side, diag, source = bufs[:5]
    terms = here[0].shape[0]
    span = pl.ds(start, stop - start)
    until = fetch(
        [
            (here[4], source),
            (here[0].at[span], own),
            (here[2], side),
            (here[1].at[span], core),
            (here[3], diag),
        ]
        + list(zip(here[5:], bufs[5:])),
        sems,
    )
    until(count)
    items = []
    for n in range(stop - start):
        items.append((info[4 + start + n], own, side, n, n))
        items.append((info[4 + terms + start + n], core, diag, n, n))
    total = add_terms(items, source, kept, 2)
    if start:
        total = total + bufs[5][...]
    if not last:
        outs[0][...] = total
        return
    image, mine, theirs, stats = outs
    half = mine.shape[0]
    field = source[0].astype(jnp.float32)
    live = live_block(field.shape, info[0] * half, info[1])
    block = jnp.where(live, own_first(total, info[0]), 0.0)
    image[...] = block
    mine[...] = block[:half].astype(jnp.bfloat16)
    theirs[...] = block[half:].astype(jnp.bfloat16)
    product = jnp.sum(field * block, keepdims=True)
    squares = jnp.sum(field * field, keepdims=True)
    quotient = product / (squares + EPS)
    resid = block - quotient * field
    rest = jnp.sum(resid * resid, keepdims=True)
    for row, value in enumerate((product, squares, rest, quotient)):
        stats[row] = jnp.broadcast_to(value, stats.shape[1:])


def merged(*stats):
    product = sum(t[0] for t in stats)
    squares = sum(t[1] for t in stats)
    quotient = product / (squares + EPS)
    rest = 0.0
    for t in stats:
        off = t[3] - quotient
        rest += t[2] + 2.0 * off * (t[0] - t[3] * t[1]) + off * off * t[1]
    return product, squares, rest, quotient


def second_kernel(entries, spans, info, *refs):
    count = 12 + 2 * len(spans)
    here, refs = refs[:count], refs[count:]
    (mine, theirs, ritz), (sems, second, kept), bufs = refs[:3], refs[3:6], refs[6:]
    stats_a, stats_b, source, *blocks = bufs[:8]
    own, core = bufs[10:12]
    pairs = list(zip(here[:8], bufs[:8]))
    before = len(pairs)
    for n, (start, stop) in enumerate(spans):
        span = pl.ds(start, stop - start)
        pairs += [
            (here[10].at[span], own.at[span]),
            (here[11].at[span], core.at[span]),
            (here[12 + 2 * n], bufs[12 + 2 * n]),
            (here[13 + 2 * n], bufs[13 + 2 * n]),
        ]
    pairs += [(here[8], mine.at[0]), (here[9], theirs.at[0])]
    until = fetch(pairs, sems)
    terms = own.shape[0]
    across, parity = info[0], info[2] % 2
    half = mine.shape[1]
    until(before)
    _, _, rest, quotient = merged(stats_a[...], stats_b[...])
    factor = lax.rsqrt(rest / entries + EPS)
    ritz[...] = quotient
    factor, quotient = factor[:1, :1], quotient[:1, :1]
    for place, block, turned in zip((0, 1, 2, 4 - parity, 3 + parity), blocks, (0, 0, 0, 0, 1)):
        image = block[...]
        if turned:
            image = jnp.concatenate([image[half:], image[:half]], axis=0)
        resid = image - quotient * source[place].astype(jnp.float32)
        second[place] = (resid * factor).astype(jnp.bfloat16)

    total = None
    for n, (start, stop) in enumerate(spans):
        until(before + 4 * (n + 1))
        items = []
        for w in range(start, stop):
            items.append((info[4 + w], own, bufs[12 + 2 * n], w, w - start))
            items.append((info[4 + terms + w], core, bufs[13 + 2 * n], w, w - start))
        part = add_terms(items, second, kept, 2)
        total = part if total is None else total + part
    total = own_first(total, across)
    live = live_block(total.shape, across * half, info[1])
    block = jnp.where(live, total, 0.0).astype(jnp.bfloat16)
    mine[1] = block[:half]
    theirs[1] = block[half:]
    until(len(pairs))


def whole_call(body, operands, out_shape, scratch, info, flops, name):
    space = pl.BlockSpec(memory_space=pltpu.VMEM)
    return pl.pallas_call(
        body,
        in_specs=[pl.BlockSpec(memory_space=pltpu.SMEM)]
        + [pl.BlockSpec(memory_space=pl.ANY)] * len(operands),
        out_specs=[space] * len(out_shape),
        out_shape=out_shape,
        scratch_shapes=scratch,
        compiler_params=pltpu.CompilerParams(vmem_limit_bytes=63 * 2**20),
        cost_estimate=pl.CostEstimate(flops=flops, bytes_accessed=flops // 256, transcendentals=0),
        name=name,
    )(info, *operands)


def room(array, count=None):
    return pltpu.VMEM((count or array.shape[0],) + array.shape[1:], array.dtype)


def on_device(psi, sector_size, left_env, right_env, term_shift):
    terms, _, slots, half, width = left_env.shape
    cell = ("contr", "mpo")
    across, core = lax.axis_index("contr"), lax.axis_index("mpo")
    me = across * 2 + core
    sectors = lax.axis_size("sector")
    cuts = [terms * part // CUTS[-1] for part in CUTS]
    spans = list(zip(cuts[:-1], cuts[1:]))

    def swap(array, flip):
        return lax.ppermute(array, cell, [(i, i ^ flip) for i in range(slots)])

    quarter = half // 2
    part = lax.dynamic_slice(
        psi[0], (1 - across, core * quarter, 0), (slots - 1, quarter, width)
    )
    part = swap(part, 2)
    shift_core = swap(term_shift, 1)
    size_here = lax.dynamic_index_in_dim(sector_size[0], me, 0, keepdims=False)
    info = jnp.concatenate(
        [jnp.stack([across, size_here, me, jnp.int32(0)]), term_shift, shift_core]
    )
    start, stop = spans[0]
    head = pack([(start, stop, 2), (start, stop, 3)], info, left_env, right_env)
    rest = [(start, stop, flip) for start, stop in spans[1:] for flip in (2, 3)]
    *tail, to_core, own_env = pack(
        rest + [(0, terms, 1), (0, terms, 0)], info, left_env, right_env, head
    )
    messages = [swap(m, 2 + i % 2) for i, m in enumerate([*head, *tail])]
    core_env = swap(to_core, 1)

    psi_mine = lax.dynamic_slice_in_dim(psi[0], across, slots - 1, axis=0)
    part_core = swap(part, 1)
    whole = jnp.concatenate(
        [
            psi_mine,
            jnp.where(core == 0, part, part_core),
            jnp.where(core == 0, part_core, part),
        ],
        axis=1,
    )
    sizes = lax.dynamic_slice_in_dim(sector_size[0], across, slots - 1, axis=0)[:, None, None]
    ids = lax.iota(jnp.int32, width)
    row_ids = (ids + across * half) % width
    live = (row_ids[None, :, None] < sizes) & (ids[None, None, :] < sizes)
    whole = jnp.where(live, whole, jnp.zeros_like(whole))
    blank = jnp.zeros_like(whole[:1])
    framed = jnp.concatenate([blank, whole, blank], axis=0)
    own = lax.dynamic_index_in_dim(whole, core, 0, keepdims=False)
    own = jnp.where(across == 0, own, lax.dynamic_index_in_dim(whole, core + 1, 0, keepdims=False))
    up = [(i, i + 1) for i in range(sectors - 1)]
    down = [(i + 1, i) for i in range(sectors - 1)]
    source = jnp.stack(
        [
            own,
            lax.ppermute(own, "sector", up),
            lax.ppermute(own, "sector", down),
            lax.dynamic_index_in_dim(framed, me - across, 0, keepdims=False),
            lax.dynamic_index_in_dim(framed, me - across + 2, 0, keepdims=False),
        ]
    )

    plain = jax.ShapeDtypeStruct((width, width), jnp.float32)
    rows = jax.ShapeDtypeStruct((half, width), jnp.bfloat16)
    tile = jax.ShapeDtypeStruct((4, 8, 128), jnp.float32)
    kept = pltpu.VMEM((2, 2 * width, width), jnp.bfloat16)
    total = []
    for index, (start, stop) in enumerate(spans):
        last = stop == terms
        size = stop - start
        operands = [own_env, core_env, *messages[2 * index : 2 * index + 2], source, *total]
        total = whole_call(
            functools.partial(first_kernel, start, stop, last),
            operands,
            [plain, rows, rows, tile] if last else [plain],
            [pltpu.SemaphoreType.DMA((len(operands),)), kept]
            + [room(m, size) for m in operands[:4]]
            + [room(m) for m in operands[4:]],
            info,
            8 * size * width**3,
            f"first_terms_{start}",
        )
    image_one, mine_one, theirs_one, stats = total

    middle = [(1, 2), (2, 1)]
    blocks = [
        image_one,
        lax.ppermute(image_one, "sector", up),
        lax.ppermute(image_one, "sector", down),
        swap(image_one, 1),
        lax.ppermute(image_one, cell, middle),
    ]
    stats = jnp.stack(merged(stats, swap(stats, 1), swap(stats, 2), swap(stats, 3)))
    flip = 1
    while flip < sectors:
        pair = lax.ppermute(stats, "sector", [(i, i ^ flip) for i in range(sectors)])
        flip *= 2
        if flip < sectors:
            stats = jnp.stack(merged(stats, pair))

    operands = [stats, pair, source, *blocks, mine_one, theirs_one, own_env, core_env, *messages]
    mine, theirs, ritz = whole_call(
        functools.partial(second_kernel, float(sectors * slots * width * width), spans),
        operands,
        [
            jax.ShapeDtypeStruct((2, half, width), jnp.bfloat16),
            jax.ShapeDtypeStruct((2, half, width), jnp.bfloat16),
            jax.ShapeDtypeStruct((8, 128), jnp.float32),
        ],
        [
            pltpu.SemaphoreType.DMA((10 + 4 * len(spans),)),
            pltpu.VMEM((5, width, width), jnp.bfloat16),
            kept,
        ]
        + [room(m) for m in operands],
        info,
        8 * terms * width**3,
        "second_terms",
    )

    got = [mine, swap(mine, 1), swap(theirs, 2)]
    got.append(swap(got[2], 1))
    flips = [me ^ v for v in range(slots)]
    images = [
        jnp.stack(
            [
                jnp.where(
                    f < 2,
                    jnp.where(f == 0, got[0][n], got[1][n]),
                    jnp.where(f == 2, got[2][n], got[3][n]),
                )
                for f in flips
            ]
        )[None]
        for n in range(2)
    ]
    return images[0], images[1], ritz[0, :1]


def solution(mesh):
    sectors = mesh.shape["sector"]
    fits = mesh.shape["contr"] == 2 and mesh.shape["mpo"] == 2
    fits = fits and sectors > 1 and sectors & (sectors - 1) == 0

    def body(psi, sector_size, left_env, right_env, term_shift):
        run = on_device if fits and psi.shape[1] == 4 else on_device_gather
        return run(psi, sector_size, left_env, right_env, term_shift)

    return jax.shard_map(
        body,
        mesh=mesh,
        in_specs=(
            P(("groups", "sector"), None, "contr", None),
            P(("groups", "sector"), None),
            P("mpo", ("groups", "sector"), None, "contr", None),
            P("mpo", ("groups", "sector"), None, None, "contr"),
            P(("groups", "mpo")),
        ),
        out_specs=(
            P(("groups", "sector"), None, "contr", None),
            P(("groups", "sector"), None, "contr", None),
            P("groups"),
        ),
        check_vma=False,
    )
```

```python
import functools

import jax
import jax.numpy as jnp
from jax import lax
from jax.experimental import pallas as pl
from jax.experimental.pallas import tpu as pltpu
from jax.sharding import PartitionSpec as P

CUTS = (0, 6, 9, 12, 13)
EPS = 1e-06


def padded(cells, sides, width):
    for axis, dim in sides:
        count = lax.axis_size(axis)
        ends = count - 1
        head = lax.slice_in_dim(cells, 0, width, axis=dim)
        tail = lax.slice_in_dim(cells, cells.shape[dim] - width, cells.shape[dim], axis=dim)
        cells = jnp.concatenate(
            [
                lax.ppermute(tail, axis, [(i, (i + 1) % count) for i in range(ends)]),
                cells,
                lax.ppermute(head, axis, [((i + 1) % count, i) for i in range(ends)]),
            ],
            axis=dim,
        )
    return cells


def on_device_gather(psi, sector_size, left_env, right_env, term_shift):
    slots = psi.shape[1]
    rows_here = psi.shape[2]
    width = psi.shape[3]
    row_ids = lax.axis_index("contr") * rows_here + lax.iota(jnp.int32, rows_here)
    col_ids = lax.iota(jnp.int32, width)
    live = sector_size[0][:, None, None]
    mask = ((row_ids[None, :, None] < live) & (col_ids[None, None, :] < live)).astype(jnp.float32)[
        None
    ]

    def apply_h(field):
        extended = padded(field, (("sector", 0),), 1)
        own = field[0]
        blank = jnp.zeros_like(own[:1])
        stacked = jnp.stack(
            [
                own,
                extended[0],
                extended[2],
                jnp.concatenate([blank, own[:-1]], 0),
                jnp.concatenate([own[1:], blank], 0),
            ]
        )
        sources = stacked[term_shift]
        inner = jnp.einsum(
            "wvrl,wvml->wvrm",
            sources,
            lax.all_gather(left_env, "contr", axis=3, tiled=True)[:, 0],
            preferred_element_type=jnp.float32,
        ).astype(jnp.bfloat16)
        partial_sum = jnp.einsum(
            "wvpr,wvrm->vpm", right_env[:, 0], inner, preferred_element_type=jnp.float32
        )
        summed = lax.psum_scatter(partial_sum, "contr", scatter_dimension=1, tiled=True)
        summed = lax.psum(summed, "mpo")
        return summed[None] * mask

    first = psi * mask.astype(jnp.bfloat16)
    image_one = apply_h(first)
    trial = first.astype(jnp.float32)
    entries = float(lax.axis_size("sector") * slots * width * width)
    product, squares = lax.psum(
        (jnp.sum(trial * image_one), jnp.sum(trial * trial)), ("sector", "contr")
    )
    ritz_value = product / (squares + EPS)
    resid = image_one - ritz_value * trial
    total_sq = lax.psum(jnp.sum(resid * resid), ("sector", "contr"))
    factor = lax.rsqrt(total_sq / entries + EPS)
    second = (resid * factor).astype(jnp.bfloat16)
    image_two = apply_h(second)
    return (
        image_one.astype(jnp.bfloat16),
        image_two.astype(jnp.bfloat16),
        jnp.reshape(ritz_value, (1,)),
    )


def live_block(shape, start, live):
    rows = (lax.broadcasted_iota(jnp.int32, shape, 0) + start) % shape[0]
    cols = lax.broadcasted_iota(jnp.int32, shape, 1)
    return (rows < live) & (cols < live)


def fetch(pairs, sems):
    copies = [pltpu.make_async_copy(x, y, sems.at[n]) for n, (x, y) in enumerate(pairs)]
    for copy in copies:
        copy.start()
    done = [0]

    def until(count):
        for copy in copies[done[0] : count]:
            copy.wait()
        done[0] = max(done[0], count)

    return until


def pack_kernel(parts, left_env, right_env, *refs):
    count = len(parts)
    refs = refs[-2 * count - 2 :]
    outs, bufs, (ins_sem, outs_sem) = refs[:count], refs[count : 2 * count], refs[-2:]
    half = right_env.shape[-1]
    width = right_env.shape[-2]
    me = lax.axis_index("contr") * 2 + lax.axis_index("mpo")
    copies = []
    for (start, stop, flip), buf in zip(parts, bufs):
        slot = me ^ flip
        span = pl.ds(start, stop - start)
        pieces = [(right_env.at[span, 0, slot], buf.at[:, pl.ds(0, width)])]
        for lane in range(width // half):
            pieces.append(
                (
                    left_env.at[span, 0, slot, :, pl.ds(lane * half, half)],
                    buf.at[:, pl.ds(width + lane * half, half)],
                )
            )
        copies.append(pieces)
    flat = [pair for pieces in copies for pair in pieces]
    until = fetch(flat, ins_sem)
    sends = [pltpu.make_async_copy(b, o, outs_sem.at[n]) for n, (b, o) in enumerate(zip(bufs, outs))]
    each = len(copies[0])
    for n, send in enumerate(sends):
        until(each * (n + 1))
        send.start()
    for send in sends:
        send.wait()


def pack(parts, left_env, right_env, after=()):
    width, half = right_env.shape[-2:]
    shapes = [(stop - start, 2 * width, half) for start, stop, _ in parts]
    out_shape = [jax.ShapeDtypeStruct(shape, jnp.bfloat16) for shape in shapes]
    size = sum(shape[0] for shape in shapes) * width * half * 8
    return pl.pallas_call(
        functools.partial(pack_kernel, parts),
        in_specs=[pl.BlockSpec(memory_space=pl.ANY)] * (2 + len(after)),
        out_specs=[pl.BlockSpec(memory_space=pl.ANY)] * len(parts),
        out_shape=out_shape,
        scratch_shapes=[pltpu.VMEM(shape, jnp.bfloat16) for shape in shapes]
        + [
            pltpu.SemaphoreType.DMA((len(parts) * (1 + width // half),)),
            pltpu.SemaphoreType.DMA((len(parts),)),
        ],
        compiler_params=pltpu.CompilerParams(vmem_limit_bytes=63 * 2**20),
        cost_estimate=pl.CostEstimate(flops=0, bytes_accessed=size, transcendentals=0),
        name=f"pack_{parts[0][0]}_{len(parts)}",
    )(left_env, right_env, *after)


def inner_block(source, near, far):
    half = near.shape[1]
    left = [
        jnp.concatenate([m[2 * half + k * half : 3 * half + k * half] for k in range(2)], axis=1)
        for m in (near, far)
    ]
    return lax.dot_general(
        source,
        jnp.concatenate(left, axis=0),
        (((1,), (1,)), ((), ())),
        preferred_element_type=jnp.float32,
    ).astype(jnp.bfloat16)


def add_terms(items, source, kept, group):
    width = source.shape[-1]
    half = width // 2
    total = None
    groups = [items[at : at + group] for at in range(0, len(items), group)]

    def inners(index):
        for k, (shift, near, far, i, j) in enumerate(groups[index]):
            kept[index % 2, k * width : (k + 1) * width, :] = inner_block(
                source[shift], near[i], far[j]
            )

    inners(0)
    for index, batch in enumerate(groups):
        if index + 1 < len(groups):
            inners(index + 1)
        right = jnp.concatenate(
            [m[n, :width] for _, near, far, i, j in batch for m, n in ((near, i), (far, j))], axis=1
        )
        part = jnp.dot(
            right,
            kept[index % 2, : len(batch) * width, :],
            preferred_element_type=jnp.float32,
        )
        total = part if total is None else total + part
    return total


def own_first(block, across):
    half = block.shape[0] // 2
    turned = jnp.concatenate([block[half:], block[:half]], axis=0)
    turned = jnp.concatenate([turned[:, half:], turned[:, :half]], axis=1)
    return jnp.where(across == 0, block, turned)


def folded(block):
    rows = jnp.sum(block.reshape(block.shape[0] // 8, 8, block.shape[1]), axis=0)
    return sum(rows[:, at : at + 128] for at in range(0, block.shape[1], 128))


def first_kernel(start, stop, last, info, *refs):
    count = 6 if start else 5
    here, refs = refs[:count], refs[count:]
    outs, (sems, kept, *bufs) = refs[: 3 if last else 1], refs[3 if last else 1 :]
    own, core, side, diag, source = bufs[:5]
    terms = here[0].shape[0]
    span = pl.ds(start, stop - start)
    until = fetch(
        [
            (here[4], source),
            (here[0].at[span], own),
            (here[2], side),
            (here[1].at[span], core),
            (here[3], diag),
        ]
        + list(zip(here[5:], bufs[5:])),
        sems,
    )
    until(count)
    items = []
    for n in range(stop - start):
        items.append((info[4 + start + n], own, side, n, n))
        items.append((info[4 + terms + start + n], core, diag, n, n))
    total = add_terms(items, source, kept, 4)
    if start:
        total = total + bufs[5][...]
    if not last:
        outs[0][...] = total
        return
    image, mine, theirs = outs
    half = mine.shape[0]
    field = source[0].astype(jnp.float32)
    live = live_block(field.shape, info[0] * half, info[1])
    block = jnp.where(live, own_first(total, info[0]), 0.0)
    image[: field.shape[0], :] = block
    mine[...] = block[:half].astype(jnp.bfloat16)
    theirs[...] = block[half:].astype(jnp.bfloat16)
    product, squares = folded(field * block), folded(field * field)
    quotient = product / (squares + EPS)
    turns = (field.shape[0] // 8, field.shape[1] // 128)
    resid = block - jnp.tile(quotient, turns) * field
    for row, value in enumerate((product, squares, folded(resid * resid), quotient)):
        at = field.shape[0] + 8 * (row // 2)
        image[at : at + 8, 128 * (row % 2) : 128 * (row % 2 + 1)] = value


def spread_kernel(mine, near, across, far, first, second):
    me = lax.axis_index("contr") * 2 + lax.axis_index("mpo")
    for flip, piece in enumerate((mine, near, across, far)):
        first[0, me ^ flip] = piece[0]
        second[0, me ^ flip] = piece[1]


def merged(a, b):
    product = a[0] + b[0]
    squares = a[1] + b[1]
    quotient = product / (squares + EPS)
    return product, squares, about(a, quotient) + about(b, quotient), quotient


def merge_tiles(a, b):
    return jnp.stack(merged(a, b))


def about(part, quotient):
    product, squares, rest, own = part
    off = own - quotient
    return rest + (2.0 * off * (product - own * squares) + off * off * squares)


def spread_kernel(mine, near, across, far, first, second):
    me = lax.axis_index("contr") * 2 + lax.axis_index("mpo")
    for flip, piece in enumerate((mine, near, across, far)):
        first[0, me ^ flip] = piece[0]
        second[0, me ^ flip] = piece[1]


def merged(*stats):
    product = sum(t[0] for t in stats)
    squares = sum(t[1] for t in stats)
    quotient = product / (squares + EPS)
    rest = 0.0
    for t in stats:
        off = t[3] - quotient
        rest += t[2] + 2.0 * off * (t[0] - t[3] * t[1]) + off * off * t[1]
    return product, squares, rest, quotient


def second_kernel(entries, spans, info, *refs):
    count = 12 + 2 * len(spans)
    here, refs = refs[:count], refs[count:]
    (mine, theirs, ritz), (sems, second, kept), bufs = refs[:3], refs[3:6], refs[6:]
    stats_a, stats_b, source, *blocks = bufs[:8]
    own, core = bufs[10:12]
    pairs = list(zip(here[:8], bufs[:8]))
    before = len(pairs)
    for n, (start, stop) in enumerate(spans):
        span = pl.ds(start, stop - start)
        pairs += [
            (here[10].at[span], own.at[span]),
            (here[11].at[span], core.at[span]),
            (here[12 + 2 * n], bufs[12 + 2 * n]),
            (here[13 + 2 * n], bufs[13 + 2 * n]),
        ]
    pairs += [(here[8], mine.at[0]), (here[9], theirs.at[0])]
    until = fetch(pairs, sems)
    terms = own.shape[0]
    across, parity, lower = info[0], info[2] % 2, info[3]
    half = mine.shape[1]
    until(before)
    parts = merged(
        [stats_a[row] for row in range(4)],
        [stats_b[row] for row in range(4)],
    )
    product, squares = (jnp.sum(part, keepdims=True) for part in parts[:2])
    quotient = product / (squares + EPS)
    factor = lax.rsqrt(jnp.sum(about(parts, quotient), keepdims=True) / entries + EPS)
    ritz[...] = quotient
    places = (0, 2 - lower, 1 + lower, 4 - parity, 3 + parity)
    for place, block, turned in zip(places, blocks, (0, 0, 0, 0, 1)):
        image = block[: 2 * half, :]
        if turned:
            image = jnp.concatenate([image[half:], image[:half]], axis=0)
        resid = image - quotient * source[place].astype(jnp.float32)
        second[place] = (resid * factor).astype(jnp.bfloat16)

    items = []
    for n, (start, stop) in enumerate(spans):
        for w in range(start, stop):
            items.append((info[4 + w], own, bufs[12 + 2 * n], w, w - start))
            items.append((info[4 + terms + w], core, bufs[13 + 2 * n], w, w - start))
    until(len(pairs) - 2)
    total = add_terms(items, second, kept, 4)
    total = own_first(total, across)
    live = live_block(total.shape, across * half, info[1])
    block = jnp.where(live, total, 0.0).astype(jnp.bfloat16)
    mine[1] = block[:half]
    theirs[1] = block[half:]
    until(len(pairs))


def whole_call(body, operands, out_shape, scratch, info, flops, name):
    space = pl.BlockSpec(memory_space=pltpu.VMEM)
    return pl.pallas_call(
        body,
        in_specs=[pl.BlockSpec(memory_space=pltpu.SMEM)]
        + [pl.BlockSpec(memory_space=pl.ANY)] * len(operands),
        out_specs=[space] * len(out_shape),
        out_shape=out_shape,
        scratch_shapes=scratch,
        compiler_params=pltpu.CompilerParams(vmem_limit_bytes=24 * 2**20),
        cost_estimate=pl.CostEstimate(flops=flops, bytes_accessed=flops // 256, transcendentals=0),
        name=name,
    )(info, *operands)


def room(array, count=None):
    return pltpu.VMEM((count or array.shape[0],) + array.shape[1:], array.dtype)


def on_device(psi, sector_size, left_env, right_env, term_shift):
    terms, _, slots, half, width = left_env.shape
    cell = ("contr", "mpo")
    across, core = lax.axis_index("contr"), lax.axis_index("mpo")
    me = across * 2 + core
    lower = lax.axis_index("sector") % 2
    sectors = lax.axis_size("sector")
    cuts = [terms * part // CUTS[-1] for part in CUTS]
    spans = list(zip(cuts[:-1], cuts[1:]))

    def swap(array, flip):
        return lax.ppermute(array, cell, [(i, i ^ flip) for i in range(slots)])

    quarter = half // 2
    part = lax.dynamic_slice(
        psi[0], (1 - across, core * quarter, 0), (slots - 1, quarter, width)
    )
    part = swap(part, 2)
    shift_core = swap(term_shift, 1)
    start, stop = spans[0]
    head = pack([(start, stop, 2), (start, stop, 3)], left_env, right_env)
    rest = [(start, stop, flip) for start, stop in spans[1:] for flip in (2, 3)]
    *tail, to_core, own_env = pack(
        rest + [(0, terms, 1), (0, terms, 0)], left_env, right_env, [*head, part]
    )
    messages = [swap(m, 2 + i % 2) for i, m in enumerate([*head, *tail])]
    core_env = swap(to_core, 1)
    size_here = lax.dynamic_index_in_dim(sector_size[0], me, 0, keepdims=False)
    info = jnp.concatenate(
        [jnp.stack([across, size_here, me, lower ^ core]), term_shift, shift_core]
    )

    psi_mine = lax.dynamic_slice_in_dim(psi[0], across, slots - 1, axis=0)
    part_core = swap(part, 1)
    whole = jnp.concatenate(
        [
            psi_mine,
            jnp.where(core == 0, part, part_core),
            jnp.where(core == 0, part_core, part),
        ],
        axis=1,
    )
    sizes = lax.dynamic_slice_in_dim(sector_size[0], across, slots - 1, axis=0)[:, None, None]
    ids = lax.iota(jnp.int32, width)
    row_ids = (ids + across * half) % width
    live = (row_ids[None, :, None] < sizes) & (ids[None, None, :] < sizes)
    whole = jnp.where(live, whole, jnp.zeros_like(whole))
    blank = jnp.zeros_like(whole[:1])
    framed = jnp.concatenate([blank, whole, blank], axis=0)
    own = lax.dynamic_index_in_dim(whole, core, 0, keepdims=False)
    own = jnp.where(across == 0, own, lax.dynamic_index_in_dim(whole, core + 1, 0, keepdims=False))
    even = [(i, i ^ 1) for i in range(sectors)]
    odd = [(i, (i - 1 ^ 1) + 1) for i in range(1, sectors - 1)]
    in_even, in_odd = lax.ppermute(own, "sector", even), lax.ppermute(own, "sector", odd)
    source = jnp.stack(
        [
            own,
            jnp.where(lower == 1, in_even, in_odd),
            jnp.where(lower == 1, in_odd, in_even),
            lax.dynamic_index_in_dim(framed, me - across, 0, keepdims=False),
            lax.dynamic_index_in_dim(framed, me - across + 2, 0, keepdims=False),
        ]
    )

    plain = jax.ShapeDtypeStruct((width, width), jnp.float32)
    sent = jax.ShapeDtypeStruct((width + 16, width), jnp.float32)
    rows = jax.ShapeDtypeStruct((half, width), jnp.bfloat16)
    kept = pltpu.VMEM((2, 4 * width, width), jnp.bfloat16)
    total = []
    for index, (start, stop) in enumerate(spans):
        last = stop == terms
        size = stop - start
        operands = [own_env, core_env, *messages[2 * index : 2 * index + 2], source, *total]
        total = whole_call(
            functools.partial(first_kernel, start, stop, last),
            operands,
            [sent, rows, rows] if last else [plain],
            [pltpu.SemaphoreType.DMA((len(operands),)), kept]
            + [room(m, size) for m in operands[:4]]
            + [room(m) for m in operands[4:]],
            info,
            8 * size * width**3,
            f"first_terms_{start}",
        )
    image_one, mine_one, theirs_one = total

    def sums_of(tail):
        tail = tail.reshape(2, 8, 2, 128)
        return tail.transpose(0, 2, 1, 3).reshape(4, 8, 128)

    near = swap(image_one, 1)
    beyond = lax.ppermute(image_one, cell, [(1, 2), (2, 1)])
    planes = ("sector", "mpo")
    turns = [
        [(2 * i + (c ^ turn), 2 * j + (c ^ turn)) for c, pairs in enumerate((even, odd)) for i, j in pairs]
        for turn in range(2)
    ]
    in_late = lax.ppermute(image_one, planes, turns[1])
    in_early = lax.ppermute(image_one, planes, turns[0])
    near, in_late, in_early, beyond = lax.optimization_barrier((near, in_late, in_early, beyond))
    even_sums = jnp.where(core == 0, in_early[width:], in_late[width:])
    stats = merge_tiles(sums_of(image_one[width:]), sums_of(even_sums))
    stats = merge_tiles(merge_tiles(stats, swap(stats, 1)), merge_tiles(swap(stats, 2), swap(stats, 3)))
    blocks = [image_one, in_early, in_late, near, beyond]
    flip = 2
    while flip < sectors:
        pair = lax.ppermute(stats, "sector", [(i, i ^ flip) for i in range(sectors)])
        flip *= 2
        if flip < sectors:
            stats = merge_tiles(stats, pair)

    operands = [stats, pair, source, *blocks, mine_one, theirs_one, own_env, core_env, *messages]
    mine, theirs, ritz = whole_call(
        functools.partial(second_kernel, float(sectors * slots * width * width), spans),
        operands,
        [
            jax.ShapeDtypeStruct((2, half, width), jnp.bfloat16),
            jax.ShapeDtypeStruct((2, half, width), jnp.bfloat16),
            jax.ShapeDtypeStruct((1, 1), jnp.float32),
        ],
        [
            pltpu.SemaphoreType.DMA((10 + 4 * len(spans),)),
            pltpu.VMEM((5, width, width), jnp.bfloat16),
            kept,
        ]
        + [room(m) for m in operands],
        info,
        8 * terms * width**3,
        "second_terms",
    )

    got = [mine, swap(mine, 1), swap(theirs, 2)]
    got.append(swap(got[2], 1))
    image = jax.ShapeDtypeStruct((1, slots, half, width), jnp.bfloat16)
    space = pl.BlockSpec(memory_space=pltpu.VMEM)
    first_image, second_image = pl.pallas_call(
        spread_kernel,
        in_specs=[space] * 4,
        out_specs=[space] * 2,
        out_shape=[image, image],
        compiler_params=pltpu.CompilerParams(vmem_limit_bytes=16 * 2**20),
        name="spread",
    )(*got)
    return first_image, second_image, ritz.reshape(1)


def solution(mesh):
    sectors = mesh.shape["sector"]
    fits = mesh.shape["contr"] == 2 and mesh.shape["mpo"] == 2
    fits = fits and sectors > 2 and sectors & (sectors - 1) == 0

    def body(psi, sector_size, left_env, right_env, term_shift):
        run = on_device if fits and psi.shape[1] == 4 else on_device_gather
        return run(psi, sector_size, left_env, right_env, term_shift)

    return jax.shard_map(
        body,
        mesh=mesh,
        in_specs=(
            P(("groups", "sector"), None, "contr", None),
            P(("groups", "sector"), None),
            P("mpo", ("groups", "sector"), None, "contr", None),
            P("mpo", ("groups", "sector"), None, None, "contr"),
            P(("groups", "mpo")),
        ),
        out_specs=(
            P(("groups", "sector"), None, "contr", None),
            P(("groups", "sector"), None, "contr", None),
            P("groups"),
        ),
        check_vma=False,
    )
```

```python
import functools

import jax
import jax.numpy as jnp
from jax import lax
from jax.experimental import pallas as pl
from jax.experimental.pallas import tpu as pltpu
from jax.sharding import PartitionSpec as P

CUTS = (0, 6, 11, 13)
EPS = 1e-06


def padded(cells, sides, width):
    for axis, dim in sides:
        count = lax.axis_size(axis)
        ends = count - 1
        head = lax.slice_in_dim(cells, 0, width, axis=dim)
        tail = lax.slice_in_dim(cells, cells.shape[dim] - width, cells.shape[dim], axis=dim)
        cells = jnp.concatenate(
            [
                lax.ppermute(tail, axis, [(i, (i + 1) % count) for i in range(ends)]),
                cells,
                lax.ppermute(head, axis, [((i + 1) % count, i) for i in range(ends)]),
            ],
            axis=dim,
        )
    return cells


def on_device_gather(psi, sector_size, left_env, right_env, term_shift):
    slots = psi.shape[1]
    rows_here = psi.shape[2]
    width = psi.shape[3]
    row_ids = lax.axis_index("contr") * rows_here + lax.iota(jnp.int32, rows_here)
    col_ids = lax.iota(jnp.int32, width)
    live = sector_size[0][:, None, None]
    mask = ((row_ids[None, :, None] < live) & (col_ids[None, None, :] < live)).astype(jnp.float32)[
        None
    ]

    def apply_h(field):
        extended = padded(field, (("sector", 0),), 1)
        own = field[0]
        blank = jnp.zeros_like(own[:1])
        stacked = jnp.stack(
            [
                own,
                extended[0],
                extended[2],
                jnp.concatenate([blank, own[:-1]], 0),
                jnp.concatenate([own[1:], blank], 0),
            ]
        )
        sources = stacked[term_shift]
        inner = jnp.einsum(
            "wvrl,wvml->wvrm",
            sources,
            lax.all_gather(left_env, "contr", axis=3, tiled=True)[:, 0],
            preferred_element_type=jnp.float32,
        ).astype(jnp.bfloat16)
        partial_sum = jnp.einsum(
            "wvpr,wvrm->vpm", right_env[:, 0], inner, preferred_element_type=jnp.float32
        )
        summed = lax.psum_scatter(partial_sum, "contr", scatter_dimension=1, tiled=True)
        summed = lax.psum(summed, "mpo")
        return summed[None] * mask

    first = psi * mask.astype(jnp.bfloat16)
    image_one = apply_h(first)
    trial = first.astype(jnp.float32)
    entries = float(lax.axis_size("sector") * slots * width * width)
    product, squares = lax.psum(
        (jnp.sum(trial * image_one), jnp.sum(trial * trial)), ("sector", "contr")
    )
    ritz_value = product / (squares + EPS)
    resid = image_one - ritz_value * trial
    total_sq = lax.psum(jnp.sum(resid * resid), ("sector", "contr"))
    factor = lax.rsqrt(total_sq / entries + EPS)
    second = (resid * factor).astype(jnp.bfloat16)
    image_two = apply_h(second)
    return (
        image_one.astype(jnp.bfloat16),
        image_two.astype(jnp.bfloat16),
        jnp.reshape(ritz_value, (1,)),
    )


def live_block(shape, start, live):
    rows = (lax.broadcasted_iota(jnp.int32, shape, 0) + start) % shape[0]
    cols = lax.broadcasted_iota(jnp.int32, shape, 1)
    return (rows < live) & (cols < live)


def fetch(pairs, sems):
    copies = [pltpu.make_async_copy(x, y, sems.at[n]) for n, (x, y) in enumerate(pairs)]
    for copy in copies:
        copy.start()
    done = [0]

    def until(count):
        for copy in copies[done[0] : count]:
            copy.wait()
        done[0] = max(done[0], count)

    return until


def pack_kernel(parts, left_env, right_env, *refs):
    count = len(parts)
    refs = refs[-2 * count - 2 :]
    outs, bufs, (ins_sem, outs_sem) = refs[:count], refs[count : 2 * count], refs[-2:]
    half = right_env.shape[-1]
    width = right_env.shape[-2]
    me = lax.axis_index("contr") * 2 + lax.axis_index("mpo")
    copies = []
    for (start, stop, flip), buf in zip(parts, bufs):
        slot = me ^ flip
        span = pl.ds(start, stop - start)
        pieces = [(right_env.at[span, 0, slot], buf.at[:, pl.ds(0, width)])]
        for lane in range(width // half):
            pieces.append(
                (
                    left_env.at[span, 0, slot, :, pl.ds(lane * half, half)],
                    buf.at[:, pl.ds(width + lane * half, half)],
                )
            )
        copies.append(pieces)
    flat = [pair for pieces in copies for pair in pieces]
    until = fetch(flat, ins_sem)
    sends = [pltpu.make_async_copy(b, o, outs_sem.at[n]) for n, (b, o) in enumerate(zip(bufs, outs))]
    each = len(copies[0])
    for n, send in enumerate(sends):
        until(each * (n + 1))
        send.start()
    for send in sends:
        send.wait()


def pack(parts, left_env, right_env, after=()):
    width, half = right_env.shape[-2:]
    shapes = [(stop - start, 2 * width, half) for start, stop, _ in parts]
    out_shape = [jax.ShapeDtypeStruct(shape, jnp.bfloat16) for shape in shapes]
    size = sum(shape[0] for shape in shapes) * width * half * 8
    return pl.pallas_call(
        functools.partial(pack_kernel, parts),
        in_specs=[pl.BlockSpec(memory_space=pl.ANY)] * (2 + len(after)),
        out_specs=[pl.BlockSpec(memory_space=pl.ANY)] * len(parts),
        out_shape=out_shape,
        scratch_shapes=[pltpu.VMEM(shape, jnp.bfloat16) for shape in shapes]
        + [
            pltpu.SemaphoreType.DMA((len(parts) * (1 + width // half),)),
            pltpu.SemaphoreType.DMA((len(parts),)),
        ],
        compiler_params=pltpu.CompilerParams(vmem_limit_bytes=63 * 2**20),
        cost_estimate=pl.CostEstimate(flops=0, bytes_accessed=size, transcendentals=0),
        name=f"pack_{parts[0][0]}_{len(parts)}",
    )(left_env, right_env, *after)


def inner_block(source, near, far):
    half = near.shape[1]
    left = [
        jnp.concatenate([m[2 * half + k * half : 3 * half + k * half] for k in range(2)], axis=1)
        for m in (near, far)
    ]
    return lax.dot_general(
        source,
        jnp.concatenate(left, axis=0),
        (((1,), (1,)), ((), ())),
        preferred_element_type=jnp.float32,
    ).astype(jnp.bfloat16)


def add_terms(items, source, kept, group):
    width = source.shape[-1]
    half = width // 2
    total = None
    groups = [items[at : at + group] for at in range(0, len(items), group)]

    def inners(index):
        for k, (shift, near, far, i, j) in enumerate(groups[index]):
            kept[index % 2, k * width : (k + 1) * width, :] = inner_block(
                source[shift], near[i], far[j]
            )

    inners(0)
    for index, batch in enumerate(groups):
        if index + 1 < len(groups):
            inners(index + 1)
        right = jnp.concatenate(
            [m[n, :width] for _, near, far, i, j in batch for m, n in ((near, i), (far, j))], axis=1
        )
        part = jnp.dot(
            right,
            kept[index % 2, : len(batch) * width, :],
            preferred_element_type=jnp.float32,
        )
        total = part if total is None else total + part
    return total


def own_first(block, across):
    half = block.shape[0] // 2
    turned = jnp.concatenate([block[half:], block[:half]], axis=0)
    turned = jnp.concatenate([turned[:, half:], turned[:, :half]], axis=1)
    return jnp.where(across == 0, block, turned)


def folded(block):
    rows = jnp.sum(block.reshape(block.shape[0] // 8, 8, block.shape[1]), axis=0)
    return sum(rows[:, at : at + 128] for at in range(0, block.shape[1], 128))


def first_kernel(start, stop, last, info, *refs):
    count = 6 if start else 5
    here, refs = refs[:count], refs[count:]
    outs, (sems, kept, *bufs) = refs[: 3 if last else 1], refs[3 if last else 1 :]
    own, core, side, diag, source = bufs[:5]
    terms = here[0].shape[0]
    span = pl.ds(start, stop - start)
    until = fetch(
        [
            (here[4], source),
            (here[0].at[span], own),
            (here[2], side),
            (here[1].at[span], core),
            (here[3], diag),
        ]
        + list(zip(here[5:], bufs[5:])),
        sems,
    )
    until(count)
    items = []
    for n in range(stop - start):
        items.append((info[4 + start + n], own, side, n, n))
        items.append((info[4 + terms + start + n], core, diag, n, n))
    total = add_terms(items, source, kept, 4)
    if start:
        total = total + bufs[5][...]
    if not last:
        outs[0][...] = total
        return
    image, mine, theirs = outs
    half = mine.shape[0]
    field = source[0].astype(jnp.float32)
    live = live_block(field.shape, info[0] * half, info[1])
    block = jnp.where(live, own_first(total, info[0]), 0.0)
    image[: field.shape[0], :] = block
    mine[...] = block[:half].astype(jnp.bfloat16)
    theirs[...] = block[half:].astype(jnp.bfloat16)
    product, squares = folded(field * block), folded(field * field)
    quotient = product / (squares + EPS)
    turns = (field.shape[0] // 8, field.shape[1] // 128)
    resid = block - jnp.tile(quotient, turns) * field
    for row, value in enumerate((product, squares, folded(resid * resid), quotient)):
        at = field.shape[0] + 8 * (row // 2)
        image[at : at + 8, 128 * (row % 2) : 128 * (row % 2 + 1)] = value


def spread_kernel(mine, near, across, far, first, second):
    me = lax.axis_index("contr") * 2 + lax.axis_index("mpo")
    for flip, piece in enumerate((mine, near, across, far)):
        first[0, me ^ flip] = piece[0]
        second[0, me ^ flip] = piece[1]


def merged(a, b):
    product = a[0] + b[0]
    squares = a[1] + b[1]
    quotient = product / (squares + EPS)
    return product, squares, about(a, quotient) + about(b, quotient), quotient


def merge_tiles(a, b):
    return jnp.stack(merged(a, b))


def about(part, quotient):
    product, squares, rest, own = part
    off = own - quotient
    return rest + (2.0 * off * (product - own * squares) + off * off * squares)


def spread_kernel(mine, near, across, far, first, second):
    me = lax.axis_index("contr") * 2 + lax.axis_index("mpo")
    for flip, piece in enumerate((mine, near, across, far)):
        first[0, me ^ flip] = piece[0]
        second[0, me ^ flip] = piece[1]


def merged(*stats):
    product = sum(t[0] for t in stats)
    squares = sum(t[1] for t in stats)
    quotient = product / (squares + EPS)
    rest = 0.0
    for t in stats:
        off = t[3] - quotient
        rest += t[2] + 2.0 * off * (t[0] - t[3] * t[1]) + off * off * t[1]
    return product, squares, rest, quotient


def second_kernel(entries, spans, info, *refs):
    count = 12 + 2 * len(spans)
    here, refs = refs[:count], refs[count:]
    (mine, theirs, ritz), (sems, second, kept), bufs = refs[:3], refs[3:6], refs[6:]
    stats_a, stats_b, source, *blocks = bufs[:8]
    own, core = bufs[10:12]
    pairs = list(zip(here[:8], bufs[:8]))
    before = len(pairs)
    for n, (start, stop) in enumerate(spans):
        span = pl.ds(start, stop - start)
        pairs += [
            (here[10].at[span], own.at[span]),
            (here[11].at[span], core.at[span]),
            (here[12 + 2 * n], bufs[12 + 2 * n]),
            (here[13 + 2 * n], bufs[13 + 2 * n]),
        ]
    pairs += [(here[8], mine.at[0]), (here[9], theirs.at[0])]
    until = fetch(pairs, sems)
    terms = own.shape[0]
    across, parity, lower = info[0], info[2] % 2, info[3]
    half = mine.shape[1]
    until(before)
    parts = merged(
        [stats_a[row] for row in range(4)],
        [stats_b[row] for row in range(4)],
    )
    product, squares = (jnp.sum(part, keepdims=True) for part in parts[:2])
    quotient = product / (squares + EPS)
    factor = lax.rsqrt(jnp.sum(about(parts, quotient), keepdims=True) / entries + EPS)
    ritz[...] = quotient
    places = (0, 2 - lower, 1 + lower, 4 - parity, 3 + parity)
    for place, block, turned in zip(places, blocks, (0, 0, 0, 0, 1)):
        image = block[: 2 * half, :]
        if turned:
            image = jnp.concatenate([image[half:], image[:half]], axis=0)
        resid = image - quotient * source[place].astype(jnp.float32)
        second[place] = (resid * factor).astype(jnp.bfloat16)

    items = []
    for n, (start, stop) in enumerate(spans):
        for w in range(start, stop):
            items.append((info[4 + w], own, bufs[12 + 2 * n], w, w - start))
            items.append((info[4 + terms + w], core, bufs[13 + 2 * n], w, w - start))
    until(len(pairs) - 2)
    total = add_terms(items, second, kept, 4)
    total = own_first(total, across)
    live = live_block(total.shape, across * half, info[1])
    block = jnp.where(live, total, 0.0).astype(jnp.bfloat16)
    mine[1] = block[:half]
    theirs[1] = block[half:]
    until(len(pairs))


def whole_call(body, operands, out_shape, scratch, info, flops, name):
    space = pl.BlockSpec(memory_space=pltpu.VMEM)
    return pl.pallas_call(
        body,
        in_specs=[pl.BlockSpec(memory_space=pltpu.SMEM)]
        + [pl.BlockSpec(memory_space=pl.ANY)] * len(operands),
        out_specs=[space] * len(out_shape),
        out_shape=out_shape,
        scratch_shapes=scratch,
        compiler_params=pltpu.CompilerParams(vmem_limit_bytes=24 * 2**20),
        cost_estimate=pl.CostEstimate(flops=flops, bytes_accessed=flops // 256, transcendentals=0),
        name=name,
    )(info, *operands)


def room(array, count=None):
    return pltpu.VMEM((count or array.shape[0],) + array.shape[1:], array.dtype)


def on_device(psi, sector_size, left_env, right_env, term_shift):
    terms, _, slots, half, width = left_env.shape
    cell = ("contr", "mpo")
    across, core = lax.axis_index("contr"), lax.axis_index("mpo")
    me = across * 2 + core
    lower = lax.axis_index("sector") % 2
    sectors = lax.axis_size("sector")
    cuts = [terms * part // CUTS[-1] for part in CUTS]
    spans = list(zip(cuts[:-1], cuts[1:]))

    def swap(array, flip):
        return lax.ppermute(array, cell, [(i, i ^ flip) for i in range(slots)])

    quarter = half // 2
    part = lax.dynamic_slice(
        psi[0], (1 - across, core * quarter, 0), (slots - 1, quarter, width)
    )
    part = swap(part, 2)
    shift_core = swap(term_shift, 1)
    start, stop = spans[0]
    head = pack([(start, stop, 2), (start, stop, 3)], left_env, right_env)
    rest = [(start, stop, flip) for start, stop in spans[1:] for flip in (2, 3)]
    *tail, to_core, own_env = pack(
        rest + [(0, terms, 1), (0, terms, 0)], left_env, right_env, [*head, part]
    )
    messages = [swap(m, 2 + i % 2) for i, m in enumerate([*head, *tail])]
    core_env = swap(to_core, 1)
    size_here = lax.dynamic_index_in_dim(sector_size[0], me, 0, keepdims=False)
    info = jnp.concatenate(
        [jnp.stack([across, size_here, me, lower ^ core]), term_shift, shift_core]
    )

    psi_mine = lax.dynamic_slice_in_dim(psi[0], across, slots - 1, axis=0)
    part_core = swap(part, 1)
    whole = jnp.concatenate(
        [
            psi_mine,
            jnp.where(core == 0, part, part_core),
            jnp.where(core == 0, part_core, part),
        ],
        axis=1,
    )
    sizes = lax.dynamic_slice_in_dim(sector_size[0], across, slots - 1, axis=0)[:, None, None]
    ids = lax.iota(jnp.int32, width)
    row_ids = (ids + across * half) % width
    live = (row_ids[None, :, None] < sizes) & (ids[None, None, :] < sizes)
    whole = jnp.where(live, whole, jnp.zeros_like(whole))
    blank = jnp.zeros_like(whole[:1])
    framed = jnp.concatenate([blank, whole, blank], axis=0)
    own = lax.dynamic_index_in_dim(whole, core, 0, keepdims=False)
    own = jnp.where(across == 0, own, lax.dynamic_index_in_dim(whole, core + 1, 0, keepdims=False))
    even = [(i, i ^ 1) for i in range(sectors)]
    odd = [(i, (i - 1 ^ 1) + 1) for i in range(1, sectors - 1)]
    in_even, in_odd = lax.ppermute(own, "sector", even), lax.ppermute(own, "sector", odd)
    source = jnp.stack(
        [
            own,
            jnp.where(lower == 1, in_even, in_odd),
            jnp.where(lower == 1, in_odd, in_even),
            lax.dynamic_index_in_dim(framed, me - across, 0, keepdims=False),
            lax.dynamic_index_in_dim(framed, me - across + 2, 0, keepdims=False),
        ]
    )

    plain = jax.ShapeDtypeStruct((width, width), jnp.float32)
    sent = jax.ShapeDtypeStruct((width + 16, width), jnp.float32)
    rows = jax.ShapeDtypeStruct((half, width), jnp.bfloat16)
    kept = pltpu.VMEM((2, 4 * width, width), jnp.bfloat16)
    total = []
    for index, (start, stop) in enumerate(spans):
        last = stop == terms
        size = stop - start
        operands = [own_env, core_env, *messages[2 * index : 2 * index + 2], source, *total]
        total = whole_call(
            functools.partial(first_kernel, start, stop, last),
            operands,
            [sent, rows, rows] if last else [plain],
            [pltpu.SemaphoreType.DMA((len(operands),)), kept]
            + [room(m, size) for m in operands[:4]]
            + [room(m) for m in operands[4:]],
            info,
            8 * size * width**3,
            f"first_terms_{start}",
        )
    image_one, mine_one, theirs_one = total

    def sums_of(tail):
        tail = tail.reshape(2, 8, 2, 128)
        return tail.transpose(0, 2, 1, 3).reshape(4, 8, 128)

    near = swap(image_one, 1)
    beyond = lax.ppermute(image_one, cell, [(1, 2), (2, 1)])
    planes = ("sector", "mpo")
    turns = [
        [(2 * i + (c ^ turn), 2 * j + (c ^ turn)) for c, pairs in enumerate((even, odd)) for i, j in pairs]
        for turn in range(2)
    ]
    in_late = lax.ppermute(image_one, planes, turns[1])
    in_early = lax.ppermute(image_one, planes, turns[0])
    near, beyond, in_late, in_early = lax.optimization_barrier((near, beyond, in_late, in_early))
    even_sums = jnp.where(core == 0, in_early[width:], in_late[width:])
    stats = merge_tiles(sums_of(image_one[width:]), sums_of(even_sums))
    stats = merge_tiles(merge_tiles(stats, swap(stats, 1)), merge_tiles(swap(stats, 2), swap(stats, 3)))
    blocks = [image_one, in_early, in_late, near, beyond]
    flip = 2
    while flip < sectors:
        pair = lax.ppermute(stats, "sector", [(i, i ^ flip) for i in range(sectors)])
        flip *= 2
        if flip < sectors:
            stats = merge_tiles(stats, pair)

    operands = [stats, pair, source, *blocks, mine_one, theirs_one, own_env, core_env, *messages]
    mine, theirs, ritz = whole_call(
        functools.partial(second_kernel, float(sectors * slots * width * width), spans),
        operands,
        [
            jax.ShapeDtypeStruct((2, half, width), jnp.bfloat16),
            jax.ShapeDtypeStruct((2, half, width), jnp.bfloat16),
            jax.ShapeDtypeStruct((1, 1), jnp.float32),
        ],
        [
            pltpu.SemaphoreType.DMA((10 + 4 * len(spans),)),
            pltpu.VMEM((5, width, width), jnp.bfloat16),
            kept,
        ]
        + [room(m) for m in operands],
        info,
        8 * terms * width**3,
        "second_terms",
    )

    got = [mine, swap(mine, 1), swap(theirs, 2)]
    got.append(swap(got[2], 1))
    image = jax.ShapeDtypeStruct((1, slots, half, width), jnp.bfloat16)
    space = pl.BlockSpec(memory_space=pltpu.VMEM)
    first_image, second_image = pl.pallas_call(
        spread_kernel,
        in_specs=[space] * 4,
        out_specs=[space] * 2,
        out_shape=[image, image],
        compiler_params=pltpu.CompilerParams(vmem_limit_bytes=16 * 2**20),
        name="spread",
    )(*got)
    return first_image, second_image, ritz.reshape(1)


def solution(mesh):
    sectors = mesh.shape["sector"]
    fits = mesh.shape["contr"] == 2 and mesh.shape["mpo"] == 2
    fits = fits and sectors > 2 and sectors & (sectors - 1) == 0

    def body(psi, sector_size, left_env, right_env, term_shift):
        run = on_device if fits and psi.shape[1] == 4 else on_device_gather
        return run(psi, sector_size, left_env, right_env, term_shift)

    return jax.shard_map(
        body,
        mesh=mesh,
        in_specs=(
            P(("groups", "sector"), None, "contr", None),
            P(("groups", "sector"), None),
            P("mpo", ("groups", "sector"), None, "contr", None),
            P("mpo", ("groups", "sector"), None, None, "contr"),
            P(("groups", "mpo")),
        ),
        out_specs=(
            P(("groups", "sector"), None, "contr", None),
            P(("groups", "sector"), None, "contr", None),
            P("groups"),
        ),
        check_vma=False,
    )
```

```python
import functools

import jax
import jax.numpy as jnp
from jax import lax
from jax.experimental import pallas as pl
from jax.experimental.pallas import tpu as pltpu
from jax.sharding import PartitionSpec as P

CUTS = (0, 6, 11, 13)
EPS = 1e-06


def padded(cells, sides, width):
    for axis, dim in sides:
        count = lax.axis_size(axis)
        ends = count - 1
        head = lax.slice_in_dim(cells, 0, width, axis=dim)
        tail = lax.slice_in_dim(cells, cells.shape[dim] - width, cells.shape[dim], axis=dim)
        cells = jnp.concatenate(
            [
                lax.ppermute(tail, axis, [(i, (i + 1) % count) for i in range(ends)]),
                cells,
                lax.ppermute(head, axis, [((i + 1) % count, i) for i in range(ends)]),
            ],
            axis=dim,
        )
    return cells


def on_device_gather(psi, sector_size, left_env, right_env, term_shift):
    slots = psi.shape[1]
    rows_here = psi.shape[2]
    width = psi.shape[3]
    row_ids = lax.axis_index("contr") * rows_here + lax.iota(jnp.int32, rows_here)
    col_ids = lax.iota(jnp.int32, width)
    live = sector_size[0][:, None, None]
    mask = ((row_ids[None, :, None] < live) & (col_ids[None, None, :] < live)).astype(jnp.float32)[
        None
    ]

    def apply_h(field):
        extended = padded(field, (("sector", 0),), 1)
        own = field[0]
        blank = jnp.zeros_like(own[:1])
        stacked = jnp.stack(
            [
                own,
                extended[0],
                extended[2],
                jnp.concatenate([blank, own[:-1]], 0),
                jnp.concatenate([own[1:], blank], 0),
            ]
        )
        sources = stacked[term_shift]
        inner = jnp.einsum(
            "wvrl,wvml->wvrm",
            sources,
            lax.all_gather(left_env, "contr", axis=3, tiled=True)[:, 0],
            preferred_element_type=jnp.float32,
        ).astype(jnp.bfloat16)
        partial_sum = jnp.einsum(
            "wvpr,wvrm->vpm", right_env[:, 0], inner, preferred_element_type=jnp.float32
        )
        summed = lax.psum_scatter(partial_sum, "contr", scatter_dimension=1, tiled=True)
        summed = lax.psum(summed, "mpo")
        return summed[None] * mask

    first = psi * mask.astype(jnp.bfloat16)
    image_one = apply_h(first)
    trial = first.astype(jnp.float32)
    entries = float(lax.axis_size("sector") * slots * width * width)
    product, squares = lax.psum(
        (jnp.sum(trial * image_one), jnp.sum(trial * trial)), ("sector", "contr")
    )
    ritz_value = product / (squares + EPS)
    resid = image_one - ritz_value * trial
    total_sq = lax.psum(jnp.sum(resid * resid), ("sector", "contr"))
    factor = lax.rsqrt(total_sq / entries + EPS)
    second = (resid * factor).astype(jnp.bfloat16)
    image_two = apply_h(second)
    return (
        image_one.astype(jnp.bfloat16),
        image_two.astype(jnp.bfloat16),
        jnp.reshape(ritz_value, (1,)),
    )


def live_block(shape, start, live):
    rows = (lax.broadcasted_iota(jnp.int32, shape, 0) + start) % shape[0]
    cols = lax.broadcasted_iota(jnp.int32, shape, 1)
    return (rows < live) & (cols < live)


def fetch(pairs, sems):
    copies = [pltpu.make_async_copy(x, y, sems.at[n]) for n, (x, y) in enumerate(pairs)]
    for copy in copies:
        copy.start()
    done = [0]

    def until(count):
        for copy in copies[done[0] : count]:
            copy.wait()
        done[0] = max(done[0], count)

    return until


def pack_kernel(parts, left_env, right_env, *refs):
    count = len(parts)
    refs = refs[-2 * count - 2 :]
    outs, bufs, (ins_sem, outs_sem) = refs[:count], refs[count : 2 * count], refs[-2:]
    half = right_env.shape[-1]
    width = right_env.shape[-2]
    me = lax.axis_index("contr") * 2 + lax.axis_index("mpo")
    copies = []
    for (start, stop, flip), buf in zip(parts, bufs):
        slot = me ^ flip
        span = pl.ds(start, stop - start)
        pieces = [(right_env.at[span, 0, slot], buf.at[:, pl.ds(0, width)])]
        for lane in range(width // half):
            pieces.append(
                (
                    left_env.at[span, 0, slot, :, pl.ds(lane * half, half)],
                    buf.at[:, pl.ds(width + lane * half, half)],
                )
            )
        copies.append(pieces)
    flat = [pair for pieces in copies for pair in pieces]
    until = fetch(flat, ins_sem)
    sends = [pltpu.make_async_copy(b, o, outs_sem.at[n]) for n, (b, o) in enumerate(zip(bufs, outs))]
    each = len(copies[0])
    for n, send in enumerate(sends):
        until(each * (n + 1))
        send.start()
    for send in sends:
        send.wait()


def pack(parts, left_env, right_env, after=()):
    width, half = right_env.shape[-2:]
    shapes = [(stop - start, 2 * width, half) for start, stop, _ in parts]
    out_shape = [jax.ShapeDtypeStruct(shape, jnp.bfloat16) for shape in shapes]
    size = sum(shape[0] for shape in shapes) * width * half * 8
    return pl.pallas_call(
        functools.partial(pack_kernel, parts),
        in_specs=[pl.BlockSpec(memory_space=pl.ANY)] * (2 + len(after)),
        out_specs=[pl.BlockSpec(memory_space=pl.ANY)] * len(parts),
        out_shape=out_shape,
        scratch_shapes=[pltpu.VMEM(shape, jnp.bfloat16) for shape in shapes]
        + [
            pltpu.SemaphoreType.DMA((len(parts) * (1 + width // half),)),
            pltpu.SemaphoreType.DMA((len(parts),)),
        ],
        compiler_params=pltpu.CompilerParams(vmem_limit_bytes=63 * 2**20),
        cost_estimate=pl.CostEstimate(flops=0, bytes_accessed=size, transcendentals=0),
        name=f"pack_{parts[0][0]}_{len(parts)}",
    )(left_env, right_env, *after)


def inner_block(source, near, far):
    half = near.shape[1]
    left = [
        jnp.concatenate([m[2 * half + k * half : 3 * half + k * half] for k in range(2)], axis=1)
        for m in (near, far)
    ]
    return lax.dot_general(
        source,
        jnp.concatenate(left, axis=0),
        (((1,), (1,)), ((), ())),
        preferred_element_type=jnp.float32,
    ).astype(jnp.bfloat16)


def add_terms(items, source, kept, group):
    width = source.shape[-1]
    half = width // 2
    total = None
    groups = [items[at : at + group] for at in range(0, len(items), group)]

    def inners(index):
        for k, (shift, near, far, i, j) in enumerate(groups[index]):
            kept[index % 2, k * width : (k + 1) * width, :] = inner_block(
                source[shift], near[i], far[j]
            )

    inners(0)
    for index, batch in enumerate(groups):
        if index + 1 < len(groups):
            inners(index + 1)
        right = jnp.concatenate(
            [m[n, :width] for _, near, far, i, j in batch for m, n in ((near, i), (far, j))], axis=1
        )
        part = jnp.dot(
            right,
            kept[index % 2, : len(batch) * width, :],
            preferred_element_type=jnp.float32,
        )
        total = part if total is None else total + part
    return total


def own_first(block, across):
    half = block.shape[0] // 2
    turned = jnp.concatenate([block[half:], block[:half]], axis=0)
    turned = jnp.concatenate([turned[:, half:], turned[:, :half]], axis=1)
    return jnp.where(across == 0, block, turned)


def folded(block):
    rows = jnp.sum(block.reshape(block.shape[0] // 8, 8, block.shape[1]), axis=0)
    return sum(rows[:, at : at + 128] for at in range(0, block.shape[1], 128))


def first_kernel(start, stop, last, info, *refs):
    here, refs = refs[:4], refs[4:]
    source, refs = refs[0], refs[1:]
    if start:
        before, refs = refs[0], refs[1:]
    outs, (sems, kept, *bufs) = refs[: 3 if last else 1], refs[3 if last else 1 :]
    own, core, side, diag = bufs
    terms = here[0].shape[0]
    span = pl.ds(start, stop - start)
    until = fetch(
        [
            (here[0].at[span], own),
            (here[2], side),
            (here[1].at[span], core),
            (here[3], diag),
        ],
        sems,
    )
    until(4)
    items = []
    for n in range(stop - start):
        items.append((info[4 + start + n], own, side, n, n))
        items.append((info[4 + terms + start + n], core, diag, n, n))
    total = add_terms(items, source, kept, 4)
    if start:
        total = total + before[...]
    if not last:
        outs[0][...] = total
        return
    image, mine, theirs = outs
    half = mine.shape[0]
    field = source[0].astype(jnp.float32)
    live = live_block(field.shape, info[0] * half, info[1])
    block = jnp.where(live, own_first(total, info[0]), 0.0)
    image[: field.shape[0], :] = block
    mine[...] = block[:half].astype(jnp.bfloat16)
    theirs[...] = block[half:].astype(jnp.bfloat16)
    product, squares = folded(field * block), folded(field * field)
    quotient = product / (squares + EPS)
    turns = (field.shape[0] // 8, field.shape[1] // 128)
    resid = block - jnp.tile(quotient, turns) * field
    for row, value in enumerate((product, squares, folded(resid * resid), quotient)):
        at = field.shape[0] + 8 * (row // 2)
        image[at : at + 8, 128 * (row % 2) : 128 * (row % 2 + 1)] = value


def spread_kernel(mine, near, across, far, first, second):
    me = lax.axis_index("contr") * 2 + lax.axis_index("mpo")
    for flip, piece in enumerate((mine, near, across, far)):
        first[0, me ^ flip] = piece[0]
        second[0, me ^ flip] = piece[1]


def merged(a, b):
    product = a[0] + b[0]
    squares = a[1] + b[1]
    quotient = product / (squares + EPS)
    return product, squares, about(a, quotient) + about(b, quotient), quotient


def merge_tiles(a, b):
    return jnp.stack(merged(a, b))


def about(part, quotient):
    product, squares, rest, own = part
    off = own - quotient
    return rest + (2.0 * off * (product - own * squares) + off * off * squares)


def spread_kernel(mine, near, across, far, first, second):
    me = lax.axis_index("contr") * 2 + lax.axis_index("mpo")
    for flip, piece in enumerate((mine, near, across, far)):
        first[0, me ^ flip] = piece[0]
        second[0, me ^ flip] = piece[1]


def merged(*stats):
    product = sum(t[0] for t in stats)
    squares = sum(t[1] for t in stats)
    quotient = product / (squares + EPS)
    rest = 0.0
    for t in stats:
        off = t[3] - quotient
        rest += t[2] + 2.0 * off * (t[0] - t[3] * t[1]) + off * off * t[1]
    return product, squares, rest, quotient


def second_kernel(entries, spans, info, *refs):
    count = 4 + 2 * len(spans)
    here, held, refs = refs[:count], refs[count : count + 8], refs[count + 8 :]
    (mine, theirs, ritz), (sems, second, kept), bufs = refs[:3], refs[3:6], refs[6:]
    stats_a, stats_b, source, *blocks = held
    own, core = bufs[:2]
    pairs = []
    for n, (start, stop) in enumerate(spans):
        span = pl.ds(start, stop - start)
        pairs += [
            (here[2].at[span], own.at[span]),
            (here[3].at[span], core.at[span]),
            (here[4 + 2 * n], bufs[2 + 2 * n]),
            (here[5 + 2 * n], bufs[3 + 2 * n]),
        ]
    pairs += [(here[0], mine.at[0]), (here[1], theirs.at[0])]
    until = fetch(pairs, sems)
    terms = own.shape[0]
    across, parity, lower = info[0], info[2] % 2, info[3]
    half = mine.shape[1]
    parts = merged(
        [stats_a[row] for row in range(4)],
        [stats_b[row] for row in range(4)],
    )
    product, squares = (jnp.sum(part, keepdims=True) for part in parts[:2])
    quotient = product / (squares + EPS)
    factor = lax.rsqrt(jnp.sum(about(parts, quotient), keepdims=True) / entries + EPS)
    ritz[...] = quotient
    places = (0, 2 - lower, 1 + lower, 4 - parity, 3 + parity)
    for place, block, turned in zip(places, blocks, (0, 0, 0, 0, 1)):
        image = block[: 2 * half, :]
        if turned:
            image = jnp.concatenate([image[half:], image[:half]], axis=0)
        resid = image - quotient * source[place].astype(jnp.float32)
        second[place] = (resid * factor).astype(jnp.bfloat16)

    items = []
    for n, (start, stop) in enumerate(spans):
        for w in range(start, stop):
            items.append((info[4 + w], own, bufs[2 + 2 * n], w, w - start))
            items.append((info[4 + terms + w], core, bufs[3 + 2 * n], w, w - start))
    until(len(pairs) - 2)
    total = add_terms(items, second, kept, 4)
    total = own_first(total, across)
    live = live_block(total.shape, across * half, info[1])
    block = jnp.where(live, total, 0.0).astype(jnp.bfloat16)
    mine[1] = block[:half]
    theirs[1] = block[half:]
    until(len(pairs))


def whole_call(body, operands, held, out_shape, scratch, info, flops, name):
    space = pl.BlockSpec(memory_space=pltpu.VMEM)
    return pl.pallas_call(
        body,
        in_specs=[pl.BlockSpec(memory_space=pltpu.SMEM)]
        + [pl.BlockSpec(memory_space=pl.ANY)] * len(operands)
        + [space] * len(held),
        out_specs=[space] * len(out_shape),
        out_shape=out_shape,
        scratch_shapes=scratch,
        compiler_params=pltpu.CompilerParams(vmem_limit_bytes=24 * 2**20),
        cost_estimate=pl.CostEstimate(flops=flops, bytes_accessed=flops // 256, transcendentals=0),
        name=name,
    )(info, *operands, *held)


def room(array, count=None):
    return pltpu.VMEM((count or array.shape[0],) + array.shape[1:], array.dtype)


def on_device(psi, sector_size, left_env, right_env, term_shift):
    terms, _, slots, half, width = left_env.shape
    cell = ("contr", "mpo")
    across, core = lax.axis_index("contr"), lax.axis_index("mpo")
    me = across * 2 + core
    lower = lax.axis_index("sector") % 2
    sectors = lax.axis_size("sector")
    cuts = [terms * part // CUTS[-1] for part in CUTS]
    spans = list(zip(cuts[:-1], cuts[1:]))

    def swap(array, flip):
        return lax.ppermute(array, cell, [(i, i ^ flip) for i in range(slots)])

    quarter = half // 2
    part = lax.dynamic_slice(
        psi[0], (1 - across, core * quarter, 0), (slots - 1, quarter, width)
    )
    part = swap(part, 2)
    shift_core = swap(term_shift, 1)
    start, stop = spans[0]
    head = pack([(start, stop, 2), (start, stop, 3)], left_env, right_env)
    rest = [(start, stop, flip) for start, stop in spans[1:] for flip in (2, 3)]
    *tail, to_core, own_env = pack(
        rest + [(0, terms, 1), (0, terms, 0)], left_env, right_env, [*head, part]
    )
    messages = [swap(m, 2 + i % 2) for i, m in enumerate([*head, *tail])]
    core_env = swap(to_core, 1)
    size_here = lax.dynamic_index_in_dim(sector_size[0], me, 0, keepdims=False)
    info = jnp.concatenate(
        [jnp.stack([across, size_here, me, lower ^ core]), term_shift, shift_core]
    )

    psi_mine = lax.dynamic_slice_in_dim(psi[0], across, slots - 1, axis=0)
    part_core = swap(part, 1)
    whole = jnp.concatenate(
        [
            psi_mine,
            jnp.where(core == 0, part, part_core),
            jnp.where(core == 0, part_core, part),
        ],
        axis=1,
    )
    sizes = lax.dynamic_slice_in_dim(sector_size[0], across, slots - 1, axis=0)[:, None, None]
    ids = lax.iota(jnp.int32, width)
    row_ids = (ids + across * half) % width
    live = (row_ids[None, :, None] < sizes) & (ids[None, None, :] < sizes)
    whole = jnp.where(live, whole, jnp.zeros_like(whole))
    blank = jnp.zeros_like(whole[:1])
    framed = jnp.concatenate([blank, whole, blank], axis=0)
    own = lax.dynamic_index_in_dim(whole, core, 0, keepdims=False)
    own = jnp.where(across == 0, own, lax.dynamic_index_in_dim(whole, core + 1, 0, keepdims=False))
    even = [(i, i ^ 1) for i in range(sectors)]
    odd = [(i, (i - 1 ^ 1) + 1) for i in range(1, sectors - 1)]
    in_even, in_odd = lax.ppermute(own, "sector", even), lax.ppermute(own, "sector", odd)
    source = jnp.stack(
        [
            own,
            jnp.where(lower == 1, in_even, in_odd),
            jnp.where(lower == 1, in_odd, in_even),
            lax.dynamic_index_in_dim(framed, me - across, 0, keepdims=False),
            lax.dynamic_index_in_dim(framed, me - across + 2, 0, keepdims=False),
        ]
    )

    plain = jax.ShapeDtypeStruct((width, width), jnp.float32)
    sent = jax.ShapeDtypeStruct((width + 16, width), jnp.float32)
    rows = jax.ShapeDtypeStruct((half, width), jnp.bfloat16)
    kept = pltpu.VMEM((2, 4 * width, width), jnp.bfloat16)
    total = []
    for index, (start, stop) in enumerate(spans):
        last = stop == terms
        size = stop - start
        operands = [own_env, core_env, *messages[2 * index : 2 * index + 2]]
        total = whole_call(
            functools.partial(first_kernel, start, stop, last),
            operands,
            [source, *total],
            [sent, rows, rows] if last else [plain],
            [pltpu.SemaphoreType.DMA((len(operands),)), kept]
            + [room(m, size) for m in operands],
            info,
            8 * size * width**3,
            f"first_terms_{start}",
        )
    image_one, mine_one, theirs_one = total

    def sums_of(tail):
        tail = tail.reshape(2, 8, 2, 128)
        return tail.transpose(0, 2, 1, 3).reshape(4, 8, 128)

    near = swap(image_one, 1)
    beyond = lax.ppermute(image_one, cell, [(1, 2), (2, 1)])
    planes = ("sector", "mpo")
    turns = [
        [(2 * i + (c ^ turn), 2 * j + (c ^ turn)) for c, pairs in enumerate((even, odd)) for i, j in pairs]
        for turn in range(2)
    ]
    in_late = lax.ppermute(image_one, planes, turns[1])
    in_early = lax.ppermute(image_one, planes, turns[0])
    near, beyond, in_late, in_early = lax.optimization_barrier((near, beyond, in_late, in_early))
    even_sums = jnp.where(core == 0, in_early[width:], in_late[width:])
    stats = merge_tiles(sums_of(image_one[width:]), sums_of(even_sums))
    stats = merge_tiles(merge_tiles(stats, swap(stats, 1)), merge_tiles(swap(stats, 2), swap(stats, 3)))
    blocks = [image_one, in_early, in_late, near, beyond]
    flip = 2
    while flip < sectors:
        pair = lax.ppermute(stats, "sector", [(i, i ^ flip) for i in range(sectors)])
        flip *= 2
        if flip < sectors:
            stats = merge_tiles(stats, pair)

    operands = [mine_one, theirs_one, own_env, core_env, *messages]
    mine, theirs, ritz = whole_call(
        functools.partial(second_kernel, float(sectors * slots * width * width), spans),
        operands,
        [stats, pair, source, *blocks],
        [
            jax.ShapeDtypeStruct((2, half, width), jnp.bfloat16),
            jax.ShapeDtypeStruct((2, half, width), jnp.bfloat16),
            jax.ShapeDtypeStruct((1, 1), jnp.float32),
        ],
        [
            pltpu.SemaphoreType.DMA((10 + 4 * len(spans),)),
            pltpu.VMEM((5, width, width), jnp.bfloat16),
            kept,
        ]
        + [room(m) for m in operands[2:]],
        info,
        8 * terms * width**3,
        "second_terms",
    )

    got = [mine, swap(mine, 1), swap(theirs, 2)]
    got.append(swap(got[2], 1))
    image = jax.ShapeDtypeStruct((1, slots, half, width), jnp.bfloat16)
    space = pl.BlockSpec(memory_space=pltpu.VMEM)
    first_image, second_image = pl.pallas_call(
        spread_kernel,
        in_specs=[space] * 4,
        out_specs=[space] * 2,
        out_shape=[image, image],
        compiler_params=pltpu.CompilerParams(vmem_limit_bytes=16 * 2**20),
        name="spread",
    )(*got)
    return first_image, second_image, ritz.reshape(1)


def solution(mesh):
    sectors = mesh.shape["sector"]
    fits = mesh.shape["contr"] == 2 and mesh.shape["mpo"] == 2
    fits = fits and sectors > 2 and sectors & (sectors - 1) == 0

    def body(psi, sector_size, left_env, right_env, term_shift):
        run = on_device if fits and psi.shape[1] == 4 else on_device_gather
        return run(psi, sector_size, left_env, right_env, term_shift)

    return jax.shard_map(
        body,
        mesh=mesh,
        in_specs=(
            P(("groups", "sector"), None, "contr", None),
            P(("groups", "sector"), None),
            P("mpo", ("groups", "sector"), None, "contr", None),
            P("mpo", ("groups", "sector"), None, None, "contr"),
            P(("groups", "mpo")),
        ),
        out_specs=(
            P(("groups", "sector"), None, "contr", None),
            P(("groups", "sector"), None, "contr", None),
            P("groups"),
        ),
        check_vma=False,
    )
```

```python
import functools

import jax
import jax.numpy as jnp
from jax import lax
from jax.experimental import pallas as pl
from jax.experimental.pallas import tpu as pltpu
from jax.sharding import PartitionSpec as P

CUTS = (0, 6, 11, 13)
EPS = 1e-06


def padded(cells, sides, width):
    for axis, dim in sides:
        count = lax.axis_size(axis)
        ends = count - 1
        head = lax.slice_in_dim(cells, 0, width, axis=dim)
        tail = lax.slice_in_dim(cells, cells.shape[dim] - width, cells.shape[dim], axis=dim)
        cells = jnp.concatenate(
            [
                lax.ppermute(tail, axis, [(i, (i + 1) % count) for i in range(ends)]),
                cells,
                lax.ppermute(head, axis, [((i + 1) % count, i) for i in range(ends)]),
            ],
            axis=dim,
        )
    return cells


def on_device_gather(psi, sector_size, left_env, right_env, term_shift):
    slots = psi.shape[1]
    rows_here = psi.shape[2]
    width = psi.shape[3]
    row_ids = lax.axis_index("contr") * rows_here + lax.iota(jnp.int32, rows_here)
    col_ids = lax.iota(jnp.int32, width)
    live = sector_size[0][:, None, None]
    mask = ((row_ids[None, :, None] < live) & (col_ids[None, None, :] < live)).astype(jnp.float32)[
        None
    ]

    def apply_h(field):
        extended = padded(field, (("sector", 0),), 1)
        own = field[0]
        blank = jnp.zeros_like(own[:1])
        stacked = jnp.stack(
            [
                own,
                extended[0],
                extended[2],
                jnp.concatenate([blank, own[:-1]], 0),
                jnp.concatenate([own[1:], blank], 0),
            ]
        )
        sources = stacked[term_shift]
        inner = jnp.einsum(
            "wvrl,wvml->wvrm",
            sources,
            lax.all_gather(left_env, "contr", axis=3, tiled=True)[:, 0],
            preferred_element_type=jnp.float32,
        ).astype(jnp.bfloat16)
        partial_sum = jnp.einsum(
            "wvpr,wvrm->vpm", right_env[:, 0], inner, preferred_element_type=jnp.float32
        )
        summed = lax.psum_scatter(partial_sum, "contr", scatter_dimension=1, tiled=True)
        summed = lax.psum(summed, "mpo")
        return summed[None] * mask

    first = psi * mask.astype(jnp.bfloat16)
    image_one = apply_h(first)
    trial = first.astype(jnp.float32)
    entries = float(lax.axis_size("sector") * slots * width * width)
    product, squares = lax.psum(
        (jnp.sum(trial * image_one), jnp.sum(trial * trial)), ("sector", "contr")
    )
    ritz_value = product / (squares + EPS)
    resid = image_one - ritz_value * trial
    total_sq = lax.psum(jnp.sum(resid * resid), ("sector", "contr"))
    factor = lax.rsqrt(total_sq / entries + EPS)
    second = (resid * factor).astype(jnp.bfloat16)
    image_two = apply_h(second)
    return (
        image_one.astype(jnp.bfloat16),
        image_two.astype(jnp.bfloat16),
        jnp.reshape(ritz_value, (1,)),
    )


def live_block(shape, start, live):
    rows = (lax.broadcasted_iota(jnp.int32, shape, 0) + start) % shape[0]
    cols = lax.broadcasted_iota(jnp.int32, shape, 1)
    return (rows < live) & (cols < live)


def fetch(pairs, sems):
    copies = [pltpu.make_async_copy(x, y, sems.at[n]) for n, (x, y) in enumerate(pairs)]
    for copy in copies:
        copy.start()
    done = [0]

    def until(count):
        for copy in copies[done[0] : count]:
            copy.wait()
        done[0] = max(done[0], count)

    return until


def pack_kernel(parts, left_env, right_env, *refs):
    count = len(parts)
    refs = refs[-2 * count - 2 :]
    outs, bufs, (ins_sem, outs_sem) = refs[:count], refs[count : 2 * count], refs[-2:]
    half = right_env.shape[-1]
    width = right_env.shape[-2]
    me = lax.axis_index("contr") * 2 + lax.axis_index("mpo")
    copies = []
    for (start, stop, flip), buf in zip(parts, bufs):
        slot = me ^ flip
        span = pl.ds(start, stop - start)
        pieces = [(right_env.at[span, 0, slot], buf.at[:, pl.ds(0, width)])]
        for lane in range(width // half):
            pieces.append(
                (
                    left_env.at[span, 0, slot, :, pl.ds(lane * half, half)],
                    buf.at[:, pl.ds(width + lane * half, half)],
                )
            )
        copies.append(pieces)
    flat = [pair for pieces in copies for pair in pieces]
    until = fetch(flat, ins_sem)
    sends = [pltpu.make_async_copy(b, o, outs_sem.at[n]) for n, (b, o) in enumerate(zip(bufs, outs))]
    each = len(copies[0])
    for n, send in enumerate(sends):
        until(each * (n + 1))
        send.start()
    for send in sends:
        send.wait()


def pack(parts, left_env, right_env, after=()):
    width, half = right_env.shape[-2:]
    shapes = [(stop - start, 2 * width, half) for start, stop, _ in parts]
    out_shape = [jax.ShapeDtypeStruct(shape, jnp.bfloat16) for shape in shapes]
    size = sum(shape[0] for shape in shapes) * width * half * 8
    return pl.pallas_call(
        functools.partial(pack_kernel, parts),
        in_specs=[pl.BlockSpec(memory_space=pl.ANY)] * (2 + len(after)),
        out_specs=[pl.BlockSpec(memory_space=pl.ANY)] * len(parts),
        out_shape=out_shape,
        scratch_shapes=[pltpu.VMEM(shape, jnp.bfloat16) for shape in shapes]
        + [
            pltpu.SemaphoreType.DMA((len(parts) * (1 + width // half),)),
            pltpu.SemaphoreType.DMA((len(parts),)),
        ],
        compiler_params=pltpu.CompilerParams(vmem_limit_bytes=63 * 2**20),
        cost_estimate=pl.CostEstimate(flops=0, bytes_accessed=size, transcendentals=0),
        name=f"pack_{parts[0][0]}_{len(parts)}",
    )(left_env, right_env, *after)


def inner_block(source, near, far):
    half = near.shape[1]
    left = [
        jnp.concatenate([m[2 * half + k * half : 3 * half + k * half] for k in range(2)], axis=1)
        for m in (near, far)
    ]
    return lax.dot_general(
        source,
        jnp.concatenate(left, axis=0),
        (((1,), (1,)), ((), ())),
        preferred_element_type=jnp.float32,
    ).astype(jnp.bfloat16)


def add_terms(items, source, kept, group):
    width = source.shape[-1]
    half = width // 2
    total = None
    groups = [items[at : at + group] for at in range(0, len(items), group)]

    def inners(index):
        for k, (shift, near, far, i, j) in enumerate(groups[index]):
            kept[index % 2, k * width : (k + 1) * width, :] = inner_block(
                source[shift], near[i], far[j]
            )

    inners(0)
    for index, batch in enumerate(groups):
        if index + 1 < len(groups):
            inners(index + 1)
        right = jnp.concatenate(
            [m[n, :width] for _, near, far, i, j in batch for m, n in ((near, i), (far, j))], axis=1
        )
        part = jnp.dot(
            right,
            kept[index % 2, : len(batch) * width, :],
            preferred_element_type=jnp.float32,
        )
        total = part if total is None else total + part
    return total


def own_first(block, across):
    half = block.shape[0] // 2
    turned = jnp.concatenate([block[half:], block[:half]], axis=0)
    turned = jnp.concatenate([turned[:, half:], turned[:, :half]], axis=1)
    return jnp.where(across == 0, block, turned)


def folded(block):
    rows = jnp.sum(block.reshape(block.shape[0] // 8, 8, block.shape[1]), axis=0)
    return sum(rows[:, at : at + 128] for at in range(0, block.shape[1], 128))


def first_kernel(start, stop, last, info, *refs):
    here, refs = refs[:4], refs[4:]
    source, refs = refs[0], refs[1:]
    if start:
        before, refs = refs[0], refs[1:]
    outs, (sems, kept, *bufs) = refs[: 3 if last else 1], refs[3 if last else 1 :]
    own, core, side, diag = bufs
    terms = here[0].shape[0]
    span = pl.ds(start, stop - start)
    until = fetch(
        [
            (here[0].at[span], own),
            (here[2], side),
            (here[1].at[span], core),
            (here[3], diag),
        ],
        sems,
    )
    until(4)
    items = []
    for n in range(stop - start):
        items.append((info[4 + start + n], own, side, n, n))
        items.append((info[4 + terms + start + n], core, diag, n, n))
    total = add_terms(items, source, kept, 4)
    if start:
        total = total + before[...]
    if not last:
        outs[0][...] = total
        return
    image, mine, theirs = outs
    half = mine.shape[0]
    field = source[0].astype(jnp.float32)
    live = live_block(field.shape, info[0] * half, info[1])
    block = jnp.where(live, own_first(total, info[0]), 0.0)
    image[: field.shape[0], :] = block
    mine[...] = block[:half].astype(jnp.bfloat16)
    theirs[...] = block[half:].astype(jnp.bfloat16)
    product, squares = folded(field * block), folded(field * field)
    quotient = product / (squares + EPS)
    turns = (field.shape[0] // 8, field.shape[1] // 128)
    resid = block - jnp.tile(quotient, turns) * field
    for row, value in enumerate((product, squares, folded(resid * resid), quotient)):
        at = field.shape[0] + 8 * (row // 2)
        image[at : at + 8, 128 * (row % 2) : 128 * (row % 2 + 1)] = value


def spread_kernel(mine, near, across, far, first, second):
    me = lax.axis_index("contr") * 2 + lax.axis_index("mpo")
    for flip, piece in enumerate((mine, near, across, far)):
        first[0, me ^ flip] = piece[0]
        second[0, me ^ flip] = piece[1]


def merged(a, b):
    product = a[0] + b[0]
    squares = a[1] + b[1]
    quotient = product / (squares + EPS)
    return product, squares, about(a, quotient) + about(b, quotient), quotient


def merge_tiles(a, b):
    return jnp.stack(merged(a, b))


def about(part, quotient):
    product, squares, rest, own = part
    off = own - quotient
    return rest + (2.0 * off * (product - own * squares) + off * off * squares)


def spread_kernel(mine, near, across, far, first, second):
    me = lax.axis_index("contr") * 2 + lax.axis_index("mpo")
    for flip, piece in enumerate((mine, near, across, far)):
        first[0, me ^ flip] = piece[0]
        second[0, me ^ flip] = piece[1]


def merged(*stats):
    product = sum(t[0] for t in stats)
    squares = sum(t[1] for t in stats)
    quotient = product / (squares + EPS)
    rest = 0.0
    for t in stats:
        off = t[3] - quotient
        rest += t[2] + 2.0 * off * (t[0] - t[3] * t[1]) + off * off * t[1]
    return product, squares, rest, quotient


def second_kernel(entries, spans, info, *refs):
    count = 4 + 2 * len(spans)
    here, held, refs = refs[:count], refs[count : count + 8], refs[count + 8 :]
    (mine, theirs, ritz), (sems, second, kept), bufs = refs[:3], refs[3:6], refs[6:]
    stats_a, stats_b, source, *blocks = held
    own, core = bufs[:2]
    pairs = []
    for n, (start, stop) in enumerate(spans):
        span = pl.ds(start, stop - start)
        pairs += [
            (here[2].at[span], own.at[span]),
            (here[3].at[span], core.at[span]),
            (here[4 + 2 * n], bufs[2 + 2 * n]),
            (here[5 + 2 * n], bufs[3 + 2 * n]),
        ]
    pairs += [(here[0], mine.at[0]), (here[1], theirs.at[0])]
    until = fetch(pairs, sems)
    terms = own.shape[0]
    across, parity, lower = info[0], info[2] % 2, info[3]
    half = mine.shape[1]
    parts = merged(
        [stats_a[row] for row in range(4)],
        [stats_b[row] for row in range(4)],
    )
    product, squares = (jnp.sum(part, keepdims=True) for part in parts[:2])
    quotient = product / (squares + EPS)
    factor = lax.rsqrt(jnp.sum(about(parts, quotient), keepdims=True) / entries + EPS)
    ritz[...] = quotient
    places = (0, 2 - lower, 1 + lower, 4 - parity, 3 + parity)
    for place, block, turned in zip(places, blocks, (0, 0, 0, 0, 1)):
        image = block[: 2 * half, :]
        if turned:
            image = jnp.concatenate([image[half:], image[:half]], axis=0)
        resid = image - quotient * source[place].astype(jnp.float32)
        second[place] = (resid * factor).astype(jnp.bfloat16)

    items = []
    for n, (start, stop) in enumerate(spans):
        for w in range(start, stop):
            items.append((info[4 + w], own, bufs[2 + 2 * n], w, w - start))
            items.append((info[4 + terms + w], core, bufs[3 + 2 * n], w, w - start))
    until(len(pairs) - 2)
    total = add_terms(items, second, kept, 4)
    total = own_first(total, across)
    live = live_block(total.shape, across * half, info[1])
    block = jnp.where(live, total, 0.0).astype(jnp.bfloat16)
    mine[1] = block[:half]
    theirs[1] = block[half:]
    until(len(pairs))


def whole_call(body, operands, held, out_shape, scratch, info, flops, name):
    space = pl.BlockSpec(memory_space=pltpu.VMEM)
    return pl.pallas_call(
        body,
        in_specs=[pl.BlockSpec(memory_space=pltpu.SMEM)]
        + [pl.BlockSpec(memory_space=pl.ANY)] * len(operands)
        + [space] * len(held),
        out_specs=[space] * len(out_shape),
        out_shape=out_shape,
        scratch_shapes=scratch,
        compiler_params=pltpu.CompilerParams(vmem_limit_bytes=24 * 2**20),
        cost_estimate=pl.CostEstimate(flops=flops, bytes_accessed=flops // 256, transcendentals=0),
        name=name,
    )(info, *operands, *held)


def room(array, count=None):
    return pltpu.VMEM((count or array.shape[0],) + array.shape[1:], array.dtype)


def on_device(psi, sector_size, left_env, right_env, term_shift):
    terms, _, slots, half, width = left_env.shape
    cell = ("contr", "mpo")
    across, core = lax.axis_index("contr"), lax.axis_index("mpo")
    me = across * 2 + core
    lower = lax.axis_index("sector") % 2
    sectors = lax.axis_size("sector")
    cuts = [terms * part // CUTS[-1] for part in CUTS]
    spans = list(zip(cuts[:-1], cuts[1:]))

    def swap(array, flip):
        return lax.ppermute(array, cell, [(i, i ^ flip) for i in range(slots)])

    quarter = half // 2
    part = lax.dynamic_slice(
        psi[0], (1 - across, core * quarter, 0), (slots - 1, quarter, width)
    )
    part = swap(part, 2)
    shift_core = swap(term_shift, 1)
    start, stop = spans[0]
    head = pack([(start, stop, 2), (start, stop, 3)], left_env, right_env)
    rest = [(start, stop, flip) for start, stop in spans[1:] for flip in (2, 3)]
    *tail, to_core, own_env = pack(
        rest + [(0, terms, 1), (0, terms, 0)], left_env, right_env, [*head, part]
    )
    messages = [swap(m, 2 + i % 2) for i, m in enumerate([*head, *tail])]
    core_env = swap(to_core, 1)
    size_here = lax.dynamic_index_in_dim(sector_size[0], me, 0, keepdims=False)
    info = jnp.concatenate(
        [jnp.stack([across, size_here, me, lower ^ core]), term_shift, shift_core]
    )

    psi_mine = lax.dynamic_slice_in_dim(psi[0], across, slots - 1, axis=0)
    part_core = swap(part, 1)
    whole = jnp.concatenate(
        [
            psi_mine,
            jnp.where(core == 0, part, part_core),
            jnp.where(core == 0, part_core, part),
        ],
        axis=1,
    )
    sizes = lax.dynamic_slice_in_dim(sector_size[0], across, slots - 1, axis=0)[:, None, None]
    ids = lax.iota(jnp.int32, width)
    row_ids = (ids + across * half) % width
    live = (row_ids[None, :, None] < sizes) & (ids[None, None, :] < sizes)
    whole = jnp.where(live, whole, jnp.zeros_like(whole))
    blank = jnp.zeros_like(whole[:1])
    framed = jnp.concatenate([blank, whole, blank], axis=0)
    own = lax.dynamic_index_in_dim(whole, core, 0, keepdims=False)
    own = jnp.where(across == 0, own, lax.dynamic_index_in_dim(whole, core + 1, 0, keepdims=False))
    even = [(i, i ^ 1) for i in range(sectors)]
    odd = [(i, (i - 1 ^ 1) + 1) for i in range(1, sectors - 1)]
    in_even, in_odd = lax.ppermute(own, "sector", even), lax.ppermute(own, "sector", odd)
    source = jnp.stack(
        [
            own,
            jnp.where(lower == 1, in_even, in_odd),
            jnp.where(lower == 1, in_odd, in_even),
            lax.dynamic_index_in_dim(framed, me - across, 0, keepdims=False),
            lax.dynamic_index_in_dim(framed, me - across + 2, 0, keepdims=False),
        ]
    )

    plain = jax.ShapeDtypeStruct((width, width), jnp.float32)
    sent = jax.ShapeDtypeStruct((width + 16, width), jnp.float32)
    rows = jax.ShapeDtypeStruct((half, width), jnp.bfloat16)
    kept = pltpu.VMEM((2, 4 * width, width), jnp.bfloat16)
    total = []
    for index, (start, stop) in enumerate(spans):
        last = stop == terms
        size = stop - start
        operands = [own_env, core_env, *messages[2 * index : 2 * index + 2]]
        total = whole_call(
            functools.partial(first_kernel, start, stop, last),
            operands,
            [source, *total],
            [sent, rows, rows] if last else [plain],
            [pltpu.SemaphoreType.DMA((len(operands),)), kept]
            + [room(m, size) for m in operands],
            info,
            8 * size * width**3,
            f"first_terms_{start}",
        )
    image_one, mine_one, theirs_one = total

    def sums_of(tail):
        tail = tail.reshape(2, 8, 2, 128)
        return tail.transpose(0, 2, 1, 3).reshape(4, 8, 128)

    near = swap(image_one, 1)
    beyond = lax.ppermute(image_one, cell, [(1, 2), (2, 1)])
    planes = ("sector", "mpo")
    turns = [
        [(2 * i + (c ^ turn), 2 * j + (c ^ turn)) for c, pairs in enumerate((even, odd)) for i, j in pairs]
        for turn in range(2)
    ]
    in_late = lax.ppermute(image_one, planes, turns[1])
    in_early = lax.ppermute(image_one, planes, turns[0])
    near, in_late, beyond, in_early = lax.optimization_barrier((near, in_late, beyond, in_early))
    even_sums = jnp.where(core == 0, in_early[width:], in_late[width:])
    stats = merge_tiles(sums_of(image_one[width:]), sums_of(even_sums))
    stats = merge_tiles(merge_tiles(stats, swap(stats, 1)), merge_tiles(swap(stats, 2), swap(stats, 3)))
    blocks = [image_one, in_early, in_late, near, beyond]
    flip = 2
    while flip < sectors:
        pair = lax.ppermute(stats, "sector", [(i, i ^ flip) for i in range(sectors)])
        flip *= 2
        if flip < sectors:
            stats = merge_tiles(stats, pair)

    operands = [mine_one, theirs_one, own_env, core_env, *messages]
    mine, theirs, ritz = whole_call(
        functools.partial(second_kernel, float(sectors * slots * width * width), spans),
        operands,
        [stats, pair, source, *blocks],
        [
            jax.ShapeDtypeStruct((2, half, width), jnp.bfloat16),
            jax.ShapeDtypeStruct((2, half, width), jnp.bfloat16),
            jax.ShapeDtypeStruct((1, 1), jnp.float32),
        ],
        [
            pltpu.SemaphoreType.DMA((10 + 4 * len(spans),)),
            pltpu.VMEM((5, width, width), jnp.bfloat16),
            kept,
        ]
        + [room(m) for m in operands[2:]],
        info,
        8 * terms * width**3,
        "second_terms",
    )

    got = [mine, swap(mine, 1), swap(theirs, 2)]
    got.append(swap(got[2], 1))
    image = jax.ShapeDtypeStruct((1, slots, half, width), jnp.bfloat16)
    space = pl.BlockSpec(memory_space=pltpu.VMEM)
    first_image, second_image = pl.pallas_call(
        spread_kernel,
        in_specs=[space] * 4,
        out_specs=[space] * 2,
        out_shape=[image, image],
        compiler_params=pltpu.CompilerParams(vmem_limit_bytes=16 * 2**20),
        name="spread",
    )(*got)
    return first_image, second_image, ritz.reshape(1)


def solution(mesh):
    sectors = mesh.shape["sector"]
    fits = mesh.shape["contr"] == 2 and mesh.shape["mpo"] == 2
    fits = fits and sectors > 2 and sectors & (sectors - 1) == 0

    def body(psi, sector_size, left_env, right_env, term_shift):
        run = on_device if fits and psi.shape[1] == 4 else on_device_gather
        return run(psi, sector_size, left_env, right_env, term_shift)

    return jax.shard_map(
        body,
        mesh=mesh,
        in_specs=(
            P(("groups", "sector"), None, "contr", None),
            P(("groups", "sector"), None),
            P("mpo", ("groups", "sector"), None, "contr", None),
            P("mpo", ("groups", "sector"), None, None, "contr"),
            P(("groups", "mpo")),
        ),
        out_specs=(
            P(("groups", "sector"), None, "contr", None),
            P(("groups", "sector"), None, "contr", None),
            P("groups"),
        ),
        check_vma=False,
    )
```

```python
import functools

import jax
import jax.numpy as jnp
from jax import lax
from jax.experimental import pallas as pl
from jax.experimental.pallas import tpu as pltpu
from jax.sharding import PartitionSpec as P

CUTS = (0, 6, 11, 13)
EPS = 1e-06


def padded(cells, sides, width):
    for axis, dim in sides:
        count = lax.axis_size(axis)
        ends = count - 1
        head = lax.slice_in_dim(cells, 0, width, axis=dim)
        tail = lax.slice_in_dim(cells, cells.shape[dim] - width, cells.shape[dim], axis=dim)
        cells = jnp.concatenate(
            [
                lax.ppermute(tail, axis, [(i, (i + 1) % count) for i in range(ends)]),
                cells,
                lax.ppermute(head, axis, [((i + 1) % count, i) for i in range(ends)]),
            ],
            axis=dim,
        )
    return cells


def on_device_gather(psi, sector_size, left_env, right_env, term_shift):
    slots = psi.shape[1]
    rows_here = psi.shape[2]
    width = psi.shape[3]
    row_ids = lax.axis_index("contr") * rows_here + lax.iota(jnp.int32, rows_here)
    col_ids = lax.iota(jnp.int32, width)
    live = sector_size[0][:, None, None]
    mask = ((row_ids[None, :, None] < live) & (col_ids[None, None, :] < live)).astype(jnp.float32)[
        None
    ]

    def apply_h(field):
        extended = padded(field, (("sector", 0),), 1)
        own = field[0]
        blank = jnp.zeros_like(own[:1])
        stacked = jnp.stack(
            [
                own,
                extended[0],
                extended[2],
                jnp.concatenate([blank, own[:-1]], 0),
                jnp.concatenate([own[1:], blank], 0),
            ]
        )
        sources = stacked[term_shift]
        inner = jnp.einsum(
            "wvrl,wvml->wvrm",
            sources,
            lax.all_gather(left_env, "contr", axis=3, tiled=True)[:, 0],
            preferred_element_type=jnp.float32,
        ).astype(jnp.bfloat16)
        partial_sum = jnp.einsum(
            "wvpr,wvrm->vpm", right_env[:, 0], inner, preferred_element_type=jnp.float32
        )
        summed = lax.psum_scatter(partial_sum, "contr", scatter_dimension=1, tiled=True)
        summed = lax.psum(summed, "mpo")
        return summed[None] * mask

    first = psi * mask.astype(jnp.bfloat16)
    image_one = apply_h(first)
    trial = first.astype(jnp.float32)
    entries = float(lax.axis_size("sector") * slots * width * width)
    product, squares = lax.psum(
        (jnp.sum(trial * image_one), jnp.sum(trial * trial)), ("sector", "contr")
    )
    ritz_value = product / (squares + EPS)
    resid = image_one - ritz_value * trial
    total_sq = lax.psum(jnp.sum(resid * resid), ("sector", "contr"))
    factor = lax.rsqrt(total_sq / entries + EPS)
    second = (resid * factor).astype(jnp.bfloat16)
    image_two = apply_h(second)
    return (
        image_one.astype(jnp.bfloat16),
        image_two.astype(jnp.bfloat16),
        jnp.reshape(ritz_value, (1,)),
    )


def live_block(shape, start, live):
    rows = (lax.broadcasted_iota(jnp.int32, shape, 0) + start) % shape[0]
    cols = lax.broadcasted_iota(jnp.int32, shape, 1)
    return (rows < live) & (cols < live)


def fetch(pairs, sems):
    copies = [pltpu.make_async_copy(x, y, sems.at[n]) for n, (x, y) in enumerate(pairs)]
    for copy in copies:
        copy.start()
    done = [0]

    def until(count):
        for copy in copies[done[0] : count]:
            copy.wait()
        done[0] = max(done[0], count)

    return until


def pack_kernel(parts, left_env, right_env, *refs):
    count = len(parts)
    refs = refs[-2 * count - 2 :]
    outs, bufs, (ins_sem, outs_sem) = refs[:count], refs[count : 2 * count], refs[-2:]
    half = right_env.shape[-1]
    width = right_env.shape[-2]
    me = lax.axis_index("contr") * 2 + lax.axis_index("mpo")
    copies = []
    for (start, stop, flip), buf in zip(parts, bufs):
        slot = me ^ flip
        span = pl.ds(start, stop - start)
        pieces = [(right_env.at[span, 0, slot], buf.at[:, pl.ds(0, width)])]
        for lane in range(width // half):
            pieces.append(
                (
                    left_env.at[span, 0, slot, :, pl.ds(lane * half, half)],
                    buf.at[:, pl.ds(width + lane * half, half)],
                )
            )
        copies.append(pieces)
    flat = [pair for pieces in copies for pair in pieces]
    until = fetch(flat, ins_sem)
    sends = [pltpu.make_async_copy(b, o, outs_sem.at[n]) for n, (b, o) in enumerate(zip(bufs, outs))]
    each = len(copies[0])
    for n, send in enumerate(sends):
        until(each * (n + 1))
        send.start()
    for send in sends:
        send.wait()


def pack(parts, left_env, right_env, after=()):
    width, half = right_env.shape[-2:]
    shapes = [(stop - start, 2 * width, half) for start, stop, _ in parts]
    out_shape = [jax.ShapeDtypeStruct(shape, jnp.bfloat16) for shape in shapes]
    size = sum(shape[0] for shape in shapes) * width * half * 8
    return pl.pallas_call(
        functools.partial(pack_kernel, parts),
        in_specs=[pl.BlockSpec(memory_space=pl.ANY)] * (2 + len(after)),
        out_specs=[pl.BlockSpec(memory_space=pl.ANY)] * len(parts),
        out_shape=out_shape,
        scratch_shapes=[pltpu.VMEM(shape, jnp.bfloat16) for shape in shapes]
        + [
            pltpu.SemaphoreType.DMA((len(parts) * (1 + width // half),)),
            pltpu.SemaphoreType.DMA((len(parts),)),
        ],
        compiler_params=pltpu.CompilerParams(vmem_limit_bytes=63 * 2**20),
        cost_estimate=pl.CostEstimate(flops=0, bytes_accessed=size, transcendentals=0),
        name=f"pack_{parts[0][0]}_{len(parts)}",
    )(left_env, right_env, *after)


def inner_block(source, near, far):
    half = near.shape[1]
    left = [
        jnp.concatenate([m[2 * half + k * half : 3 * half + k * half] for k in range(2)], axis=1)
        for m in (near, far)
    ]
    return lax.dot_general(
        source,
        jnp.concatenate(left, axis=0),
        (((1,), (1,)), ((), ())),
        preferred_element_type=jnp.float32,
    ).astype(jnp.bfloat16)


def add_terms(items, source, kept, group):
    width = source.shape[-1]
    half = width // 2
    total = None
    groups = [items[at : at + group] for at in range(0, len(items), group)]

    def inners(index):
        for k, (shift, near, far, i, j) in enumerate(groups[index]):
            kept[index % 2, k * width : (k + 1) * width, :] = inner_block(
                source[shift], near[i], far[j]
            )

    inners(0)
    for index, batch in enumerate(groups):
        if index + 1 < len(groups):
            inners(index + 1)
        right = jnp.concatenate(
            [m[n, :width] for _, near, far, i, j in batch for m, n in ((near, i), (far, j))], axis=1
        )
        part = jnp.dot(
            right,
            kept[index % 2, : len(batch) * width, :],
            preferred_element_type=jnp.float32,
        )
        total = part if total is None else total + part
    return total


def own_first(block, across):
    half = block.shape[0] // 2
    turned = jnp.concatenate([block[half:], block[:half]], axis=0)
    turned = jnp.concatenate([turned[:, half:], turned[:, :half]], axis=1)
    return jnp.where(across == 0, block, turned)


def folded(block):
    rows = jnp.sum(block.reshape(block.shape[0] // 8, 8, block.shape[1]), axis=0)
    return sum(rows[:, at : at + 128] for at in range(0, block.shape[1], 128))


def first_kernel(start, stop, last, info, *refs):
    here, refs = refs[:4], refs[4:]
    source, refs = refs[0], refs[1:]
    if start:
        before, refs = refs[0], refs[1:]
    outs, (sems, kept, *bufs) = refs[: 3 if last else 1], refs[3 if last else 1 :]
    own, core, side, diag = bufs
    terms = here[0].shape[0]
    span = pl.ds(start, stop - start)
    until = fetch(
        [
            (here[0].at[span], own),
            (here[2], side),
            (here[1].at[span], core),
            (here[3], diag),
        ],
        sems,
    )
    until(4)
    items = []
    for n in range(stop - start):
        items.append((info[4 + start + n], own, side, n, n))
        items.append((info[4 + terms + start + n], core, diag, n, n))
    total = add_terms(items, source, kept, 4)
    if start:
        total = total + before[...]
    if not last:
        outs[0][...] = total
        return
    image, mine, theirs = outs
    half = mine.shape[0]
    field = source[0].astype(jnp.float32)
    live = live_block(field.shape, info[0] * half, info[1])
    block = jnp.where(live, own_first(total, info[0]), 0.0)
    image[: field.shape[0], :] = block
    mine[...] = block[:half].astype(jnp.bfloat16)
    theirs[...] = block[half:].astype(jnp.bfloat16)
    product, squares = folded(field * block), folded(field * field)
    quotient = product / (squares + EPS)
    turns = (field.shape[0] // 8, field.shape[1] // 128)
    resid = block - jnp.tile(quotient, turns) * field
    for row, value in enumerate((product, squares, folded(resid * resid), quotient)):
        at = field.shape[0] + 8 * (row // 2)
        image[at : at + 8, 128 * (row % 2) : 128 * (row % 2 + 1)] = value


def spread_kernel(mine, near, across, far, first, second):
    me = lax.axis_index("contr") * 2 + lax.axis_index("mpo")
    for flip, piece in enumerate((mine, near, across, far)):
        first[0, me ^ flip] = piece[0]
        second[0, me ^ flip] = piece[1]


def merged(a, b):
    product = a[0] + b[0]
    squares = a[1] + b[1]
    quotient = product / (squares + EPS)
    return product, squares, about(a, quotient) + about(b, quotient), quotient


def merge_tiles(a, b):
    return jnp.stack(merged(a, b))


def about(part, quotient):
    product, squares, rest, own = part
    off = own - quotient
    return rest + (2.0 * off * (product - own * squares) + off * off * squares)


def spread_kernel(*refs):
    me = lax.axis_index("contr") * 2 + lax.axis_index("mpo")
    for flip in range(4):
        refs[8][0, me ^ flip] = refs[flip][...]
        refs[9][0, me ^ flip] = refs[4 + flip][...]


def merged(*stats):
    product = sum(t[0] for t in stats)
    squares = sum(t[1] for t in stats)
    quotient = product / (squares + EPS)
    rest = 0.0
    for t in stats:
        off = t[3] - quotient
        rest += t[2] + 2.0 * off * (t[0] - t[3] * t[1]) + off * off * t[1]
    return product, squares, rest, quotient


def second_kernel(entries, spans, info, *refs):
    count = 2 + 2 * len(spans)
    here, held, refs = refs[:count], refs[count : count + 8], refs[count + 8 :]
    (mine, theirs, ritz), (sems, second, kept), bufs = refs[:3], refs[3:6], refs[6:]
    stats_a, stats_b, source, *blocks = held
    own, core = bufs[:2]
    pairs = []
    for n, (start, stop) in enumerate(spans):
        span = pl.ds(start, stop - start)
        pairs += [
            (here[0].at[span], own.at[span]),
            (here[1].at[span], core.at[span]),
            (here[2 + 2 * n], bufs[2 + 2 * n]),
            (here[3 + 2 * n], bufs[3 + 2 * n]),
        ]
    until = fetch(pairs, sems)
    terms = own.shape[0]
    across, parity, lower = info[0], info[2] % 2, info[3]
    half = mine.shape[0]
    parts = merged(
        [stats_a[row] for row in range(4)],
        [stats_b[row] for row in range(4)],
    )
    product, squares = (jnp.sum(part, keepdims=True) for part in parts[:2])
    quotient = product / (squares + EPS)
    factor = lax.rsqrt(jnp.sum(about(parts, quotient), keepdims=True) / entries + EPS)
    ritz[...] = quotient
    places = (0, 2 - lower, 1 + lower, 4 - parity, 3 + parity)
    for place, block, turned in zip(places, blocks, (0, 0, 0, 0, 1)):
        image = block[: 2 * half, :]
        if turned:
            image = jnp.concatenate([image[half:], image[:half]], axis=0)
        resid = image - quotient * source[place].astype(jnp.float32)
        second[place] = (resid * factor).astype(jnp.bfloat16)

    items = []
    for n, (start, stop) in enumerate(spans):
        for w in range(start, stop):
            items.append((info[4 + w], own, bufs[2 + 2 * n], w, w - start))
            items.append((info[4 + terms + w], core, bufs[3 + 2 * n], w, w - start))
    until(len(pairs))
    total = add_terms(items, second, kept, 4)
    total = own_first(total, across)
    live = live_block(total.shape, across * half, info[1])
    block = jnp.where(live, total, 0.0).astype(jnp.bfloat16)
    mine[...] = block[:half]
    theirs[...] = block[half:]


def whole_call(body, operands, held, out_shape, scratch, info, flops, name):
    space = pl.BlockSpec(memory_space=pltpu.VMEM)
    return pl.pallas_call(
        body,
        in_specs=[pl.BlockSpec(memory_space=pltpu.SMEM)]
        + [pl.BlockSpec(memory_space=pl.ANY)] * len(operands)
        + [space] * len(held),
        out_specs=[space] * len(out_shape),
        out_shape=out_shape,
        scratch_shapes=scratch,
        compiler_params=pltpu.CompilerParams(vmem_limit_bytes=24 * 2**20),
        cost_estimate=pl.CostEstimate(flops=flops, bytes_accessed=flops // 256, transcendentals=0),
        name=name,
    )(info, *operands, *held)


def room(array, count=None):
    return pltpu.VMEM((count or array.shape[0],) + array.shape[1:], array.dtype)


def on_device(psi, sector_size, left_env, right_env, term_shift):
    terms, _, slots, half, width = left_env.shape
    cell = ("contr", "mpo")
    across, core = lax.axis_index("contr"), lax.axis_index("mpo")
    me = across * 2 + core
    lower = lax.axis_index("sector") % 2
    sectors = lax.axis_size("sector")
    cuts = [terms * part // CUTS[-1] for part in CUTS]
    spans = list(zip(cuts[:-1], cuts[1:]))

    def swap(array, flip):
        return lax.ppermute(array, cell, [(i, i ^ flip) for i in range(slots)])

    quarter = half // 2
    part = lax.dynamic_slice(
        psi[0], (1 - across, core * quarter, 0), (slots - 1, quarter, width)
    )
    part = swap(part, 2)
    shift_core = swap(term_shift, 1)
    start, stop = spans[0]
    head = pack([(start, stop, 2), (start, stop, 3)], left_env, right_env)
    rest = [(start, stop, flip) for start, stop in spans[1:] for flip in (2, 3)]
    *tail, to_core, own_env = pack(
        rest + [(0, terms, 1), (0, terms, 0)], left_env, right_env, [*head, part]
    )
    messages = [swap(m, 2 + i % 2) for i, m in enumerate([*head, *tail])]
    core_env = swap(to_core, 1)
    size_here = lax.dynamic_index_in_dim(sector_size[0], me, 0, keepdims=False)
    info = jnp.concatenate(
        [jnp.stack([across, size_here, me, lower ^ core]), term_shift, shift_core]
    )

    psi_mine = lax.dynamic_slice_in_dim(psi[0], across, slots - 1, axis=0)
    part_core = swap(part, 1)
    whole = jnp.concatenate(
        [
            psi_mine,
            jnp.where(core == 0, part, part_core),
            jnp.where(core == 0, part_core, part),
        ],
        axis=1,
    )
    sizes = lax.dynamic_slice_in_dim(sector_size[0], across, slots - 1, axis=0)[:, None, None]
    ids = lax.iota(jnp.int32, width)
    row_ids = (ids + across * half) % width
    live = (row_ids[None, :, None] < sizes) & (ids[None, None, :] < sizes)
    whole = jnp.where(live, whole, jnp.zeros_like(whole))
    blank = jnp.zeros_like(whole[:1])
    framed = jnp.concatenate([blank, whole, blank], axis=0)
    own = lax.dynamic_index_in_dim(whole, core, 0, keepdims=False)
    own = jnp.where(across == 0, own, lax.dynamic_index_in_dim(whole, core + 1, 0, keepdims=False))
    even = [(i, i ^ 1) for i in range(sectors)]
    odd = [(i, (i - 1 ^ 1) + 1) for i in range(1, sectors - 1)]
    in_even, in_odd = lax.ppermute(own, "sector", even), lax.ppermute(own, "sector", odd)
    source = jnp.stack(
        [
            own,
            jnp.where(lower == 1, in_even, in_odd),
            jnp.where(lower == 1, in_odd, in_even),
            lax.dynamic_index_in_dim(framed, me - across, 0, keepdims=False),
            lax.dynamic_index_in_dim(framed, me - across + 2, 0, keepdims=False),
        ]
    )

    plain = jax.ShapeDtypeStruct((width, width), jnp.float32)
    sent = jax.ShapeDtypeStruct((width + 16, width), jnp.float32)
    rows = jax.ShapeDtypeStruct((half, width), jnp.bfloat16)
    kept = pltpu.VMEM((2, 4 * width, width), jnp.bfloat16)
    total = []
    for index, (start, stop) in enumerate(spans):
        last = stop == terms
        size = stop - start
        operands = [own_env, core_env, *messages[2 * index : 2 * index + 2]]
        total = whole_call(
            functools.partial(first_kernel, start, stop, last),
            operands,
            [source, *total],
            [sent, rows, rows] if last else [plain],
            [pltpu.SemaphoreType.DMA((len(operands),)), kept]
            + [room(m, size) for m in operands],
            info,
            8 * size * width**3,
            f"first_terms_{start}",
        )
    image_one, mine_one, theirs_one = total

    def sums_of(tail):
        tail = tail.reshape(2, 8, 2, 128)
        return tail.transpose(0, 2, 1, 3).reshape(4, 8, 128)

    near = swap(image_one, 1)
    beyond = lax.ppermute(image_one, cell, [(1, 2), (2, 1)])
    planes = ("sector", "mpo")
    turns = [
        [(2 * i + (c ^ turn), 2 * j + (c ^ turn)) for c, pairs in enumerate((even, odd)) for i, j in pairs]
        for turn in range(2)
    ]
    in_late = lax.ppermute(image_one, planes, turns[1])
    in_early = lax.ppermute(image_one, planes, turns[0])
    in_early, beyond, in_late, near = lax.optimization_barrier((in_early, beyond, in_late, near))
    even_sums = jnp.where(core == 0, in_early[width:], in_late[width:])
    stats = merge_tiles(sums_of(image_one[width:]), sums_of(even_sums))
    stats = merge_tiles(merge_tiles(stats, swap(stats, 1)), merge_tiles(swap(stats, 2), swap(stats, 3)))
    blocks = [image_one, in_early, in_late, near, beyond]
    flip = 2
    while flip < sectors:
        pair = lax.ppermute(stats, "sector", [(i, i ^ flip) for i in range(sectors)])
        flip *= 2
        if flip < sectors:
            stats = merge_tiles(stats, pair)

    operands = [own_env, core_env, *messages]
    mine, theirs, ritz = whole_call(
        functools.partial(second_kernel, float(sectors * slots * width * width), spans),
        operands,
        [stats, pair, source, *blocks],
        [
            rows,
            rows,
            jax.ShapeDtypeStruct((1, 1), jnp.float32),
        ],
        [
            pltpu.SemaphoreType.DMA((10 + 4 * len(spans),)),
            pltpu.VMEM((5, width, width), jnp.bfloat16),
            kept,
        ]
        + [room(m) for m in operands],
        info,
        8 * terms * width**3,
        "second_terms",
    )

    got = []
    for near_half, far_half in ((mine_one, theirs_one), (mine, theirs)):
        arrived = swap(far_half, 2)
        got += [near_half, swap(near_half, 1), arrived, swap(arrived, 1)]
    image = jax.ShapeDtypeStruct((1, slots, half, width), jnp.bfloat16)
    space = pl.BlockSpec(memory_space=pltpu.VMEM)
    first_image, second_image = pl.pallas_call(
        spread_kernel,
        in_specs=[space] * 8,
        out_specs=[space] * 2,
        out_shape=[image, image],
        compiler_params=pltpu.CompilerParams(vmem_limit_bytes=16 * 2**20),
        name="spread",
    )(*got)
    return first_image, second_image, ritz.reshape(1)


def solution(mesh):
    sectors = mesh.shape["sector"]
    fits = mesh.shape["contr"] == 2 and mesh.shape["mpo"] == 2
    fits = fits and sectors > 2 and sectors & (sectors - 1) == 0

    def body(psi, sector_size, left_env, right_env, term_shift):
        run = on_device if fits and psi.shape[1] == 4 else on_device_gather
        return run(psi, sector_size, left_env, right_env, term_shift)

    return jax.shard_map(
        body,
        mesh=mesh,
        in_specs=(
            P(("groups", "sector"), None, "contr", None),
            P(("groups", "sector"), None),
            P("mpo", ("groups", "sector"), None, "contr", None),
            P("mpo", ("groups", "sector"), None, None, "contr"),
            P(("groups", "mpo")),
        ),
        out_specs=(
            P(("groups", "sector"), None, "contr", None),
            P(("groups", "sector"), None, "contr", None),
            P("groups"),
        ),
        check_vma=False,
    )
```
